128 devices in a mesh: blk: 8 (over z_lo, y), group: 16 (over x, z_hi, core).
Axes of the slice: x: 4, y: 4, z: 4 (z_hi: 2, z_lo: 2; z = z_hi * 2 + z_lo), core: 2. Of those that a mesh axis runs over, the one named last changes fastest.
Arguments:
- micrograph: bfloat16 [3072, 6144], P('blk', 'group'), may hold values from -6 to 6
- templates: bfloat16 [8, 384, 384], P('blk'), may hold values from -450 to 450
- ref_bank: bfloat16 [128, 384, 384], P('group'), may hold values from -0.015625 to 0.015625
- peak_offsets: int32 [2048, 2], P(('blk', 'group')), may hold values from 0 to 383
- peak_template: int32 [2048], P(('blk', 'group')), may hold values from 0 to 7
- owners: int32 [2048, 1], P(('blk', 'group')), may hold values from 0 to 15; in each aligned block of 16 rows (0 to 15, 16 to 31, ...) at most 2 rows name the same one
Outputs:
- mip: float32 [3072, 6144], P('blk', 'group')
- zmap: float32 [3072, 6144], P('blk', 'group')
- refined: float32 [2048, 9], P(('blk', 'group'))
The draws below stay inside these ranges and needn't reach their ends.
Inputs may be any that keep to these rules, and one draw needn't show every extreme that they name: `owners`: among the candidates of one device no owner is named more than 2 times.
All inputs are finite; a program needn't handle non-finite values.
Results may differ from the reference program's by a relative error of at most 0.013.
Values may be sent and summed in bfloat16 or wider, within the bound.
No kernel may reach another device: no remote copies, remote signals or barrier semaphores. Data moves between devices by JAX's collectives and lax.ppermute only.
A program may use at most 192 MiB of HBM per device.

```python
import math
import jax
import jax.numpy as jnp
import numpy as np
from jax import lax

L = 384
CANDS_DEV = 16
CAP = 2
REF_DEV = 8
TEMPLATES = 8
OWNERS = 16
REFS = 128
CANDIDATES = 2048
HEIGHT = 3072
WIDTH = 6144
N_BLK = 8
N_GROUP = 16


def draw_templates(key, part):
    key = jax.random.fold_in(key, 11)
    first, second, third, fourth = jax.random.split(key, 4)
    base = jnp.clip(jax.random.normal(first, (TEMPLATES, L, L), jnp.float32), -4.0, 4.0)
    top = math.log(10.0)
    rows = jnp.exp(jax.random.uniform(second, (TEMPLATES, L, 1), jnp.float32, 0.0, top))
    cols = jnp.exp(jax.random.uniform(third, (TEMPLATES, 1, L), jnp.float32, 0.0, top))
    offset = jax.random.uniform(fourth, (TEMPLATES, L, 1), jnp.float32, -3.0, 3.0)
    return (base * rows * cols + offset).astype(jnp.bfloat16)


def with_ends(array, rng, least, top_value):
    extent = array.shape
    place = [jax.random.randint(jax.random.fold_in(rng, axis), (), 0, extent[axis]) for axis in range(len(extent))]
    array = array.at[tuple(place)].set(least)
    longest = extent.index(max(extent))
    place[longest] = (place[longest] + 1) % extent[longest]
    return array.at[tuple(place)].set(top_value)


def level_of(own_key, shape, cuts, smallest, top_value):
    gain = 1.0
    for dim, blocks in cuts:
        steps = jax.random.uniform(jax.random.fold_in(jax.random.fold_in(own_key, 6), dim), (blocks,), jnp.float32, smallest / len(cuts), top_value / len(cuts))
        gain = gain * jnp.repeat(jnp.exp(steps), shape[dim] // blocks).reshape((-1,) + (1,) * (len(shape) - 1 - dim))
    return gain


def assign_block(own_key, own, number, rows, number_of, top, bound, slope):
    ranking = jax.random.permutation(own_key, number_of)
    packed, ordinary = portions_of(number_of, rows * top, bound, slope, True), portions_of(number_of, rows * top, bound, slope, False)
    places = jnp.arange(number_of)

    def named(sizes, rotation):
        used = int((sizes > 0).sum())
        fixed = max(1, used // 4)
        moved = fixed + (places - fixed + rotation * (used - fixed)) % max(1, number_of - fixed)
        return jnp.zeros((number_of,), jnp.int32).at[ranking[jnp.where(places < fixed, places, moved)]].set(jnp.asarray(sizes, jnp.int32))

    sizes = jnp.where(number % 4 == 0, named(packed, number // 4), named(ordinary, number - number // 4 - 1))
    mixed = jax.random.permutation(jax.random.fold_in(own, 3), number_of)
    donor, sink = mixed[0:number_of // 2 * 2:2], mixed[1:number_of // 2 * 2:2]
    room = jnp.minimum(sizes[donor] - 1, bound - sizes[sink]) // 2
    room = jnp.where((donor == ranking[0]) | (sink == ranking[0]) | (sizes[sink] == 0), 0, jnp.maximum(room, 0))
    moved = jax.random.randint(jax.random.fold_in(own, 4), (number_of // 2,), 0, 1 << 20) % (room + 1)
    sizes = sizes.at[donor].add(-moved).at[sink].add(moved)
    labels = jnp.searchsorted(jnp.cumsum(sizes), jnp.arange(rows * top), side="right").astype(jnp.int32)
    grid = labels.reshape(top, rows).T
    grid = grid[jax.random.permutation(jax.random.fold_in(own, 1), rows)]
    rotation = jax.random.randint(jax.random.fold_in(own, 2), (rows, 1), 0, top)
    return jnp.take_along_axis(grid, (jnp.arange(top)[None, :] + rotation) % top, axis=1)


def portions_of(amount, total, bound, skew, full):
    weights = [(1 << 20) // math.isqrt(standing ** skew) + 1 for standing in range(1, amount + 1)]
    largest = bound if full else min(bound, max(-(-total // amount), total * weights[0] // sum(weights)))
    least = 1 if total - largest >= amount - 1 else 0
    given, spare = [largest] + [least] * (amount - 1), total - largest - least * (amount - 1)
    while spare > 0:
        free = [i for i in range(1, amount) if given[i] < largest] or [i for i in range(1, amount) if given[i] < bound]
        whole, budget = sum([weights[i] for i in free]), spare
        for i in free:
            addition = min(bound - given[i], max(1, budget * weights[i] // whole), spare)
            given[i] = given[i] + addition
            spare = spare - addition
    return np.array(given)


def bell_draw(key, extent, scale, reach, cuts=(), held_as=jnp.bfloat16):
    entries = scale * jax.random.normal(key, extent, jnp.float32)
    if cuts:
        entries = entries * level_of(key, extent, cuts, -0.22, 0.18)
    return jnp.clip(entries, -reach, reach).astype(held_as)


def setup_inputs(seed: int = 0) -> dict:
    key_of = jax.random.split(jax.random.key(seed), 7)
    micrograph = bell_draw(key_of[0], (HEIGHT, WIDTH), 1.0, 6.0, ((0, 8), (1, 16)))
    templates = draw_templates(jax.random.fold_in(key_of[6], 71), 0)
    ref_bank = bell_draw(key_of[2], (REFS, L, L), (L * L) ** -0.5, 0.015625, ((0, 16),))
    peak_offsets = with_ends(jax.random.randint(key_of[3], (CANDIDATES, 2), 0, L), jax.random.fold_in(key_of[3], 1), 0, L - 1).astype(jnp.int32)
    peak_template = with_ends(jax.random.randint(key_of[4], (CANDIDATES,), 0, REF_DEV), jax.random.fold_in(key_of[4], 1), 0, REF_DEV - 1).astype(jnp.int32)
    owners_keys = jax.random.split(jax.random.fold_in(key_of[5], 1), CANDIDATES // CANDS_DEV)
    owners_turns = jax.random.permutation(jax.random.fold_in(key_of[5], 3), CANDIDATES // CANDS_DEV)
    owners = jax.vmap(lambda own, number: assign_block(jax.random.fold_in(key_of[5], 2), own, number, CANDS_DEV, OWNERS, 1, CAP, 2))(owners_keys, owners_turns).reshape((CANDIDATES, 1))
    return {"micrograph": micrograph, "templates": templates, "ref_bank": ref_bank, "peak_offsets": peak_offsets, "peak_template": peak_template, "owners": owners}


def tables(size):
    index = jnp.arange(size, dtype=jnp.int32)
    turned = index[:, None] * index[None, :] % size
    angle = turned.astype(jnp.float32) * (2.0 * math.pi / size)
    return (jnp.cos(angle).astype(jnp.bfloat16), jnp.sin(angle).astype(jnp.bfloat16))

def normalize(stack):
    values = stack.astype(jnp.float32)
    centre = lax.optimization_barrier(jnp.mean(values, axis=(1, 2), keepdims=True))
    spread = values - centre
    power = lax.optimization_barrier(jnp.mean(spread * spread, axis=(1, 2), keepdims=True))
    size = stack.shape[-1]
    return (spread / (size * jnp.sqrt(power + 1e-06))).astype(jnp.bfloat16)

def spectrum(image, cosine, sine):
    size = image.shape[0]
    forward = jnp.concatenate([cosine, -sine], 0)
    first = jnp.dot(forward, image, preferred_element_type=jnp.float32).astype(jnp.bfloat16)
    second = jnp.dot(first, jnp.concatenate([cosine, sine], 1), preferred_element_type=jnp.float32)
    real_part = second[:size, :size] + second[size:, size:]
    imag_part = second[size:, :size] - second[:size, size:]
    return jnp.concatenate([real_part, imag_part], 0).astype(jnp.bfloat16)

def correlate(tile_spec, tmpl_spec, cosine, sine):
    size = cosine.shape[0]
    tile_real = tile_spec[:size].astype(jnp.float32)
    tile_imag = tile_spec[size:].astype(jnp.float32)
    tmpl_real = tmpl_spec[:size].astype(jnp.float32)
    tmpl_imag = tmpl_spec[size:].astype(jnp.float32)
    product = jnp.concatenate([tile_real * tmpl_real + tile_imag * tmpl_imag, tile_imag * tmpl_real - tile_real * tmpl_imag], 0).astype(jnp.bfloat16)
    inverse = jnp.concatenate([jnp.concatenate([cosine, -sine], 1), jnp.concatenate([sine, cosine], 1)], 0)
    back = jnp.dot(inverse, product, preferred_element_type=jnp.float32).astype(jnp.bfloat16)
    joined = jnp.concatenate([back[:size], back[size:]], 1)
    forward = jnp.concatenate([cosine, -sine], 0)
    return jnp.dot(joined, forward, preferred_element_type=jnp.float32) * (1.0 / (size * size))

def accumulate(stats, corr):
    return (jnp.maximum(stats[0], corr), stats[1] + corr, stats[2] + corr * corr)

def finish(stats, count):
    mean = stats[1] / count
    var = stats[2] / count - mean * mean
    return (stats[0], (stats[0] - mean) / jnp.sqrt(jnp.maximum(var, 0.25)))

def cut_patch(tile, offsets):
    size = tile.shape[0]
    doubled = jnp.tile(tile, (2, 2))
    return lax.dynamic_slice(doubled, (offsets[0].astype(jnp.int32), offsets[1].astype(jnp.int32)), (size, size))

def score_shifts(flat, bank):
    results = []
    for row_shift in (-1, 0, 1):
        for col_shift in (-1, 0, 1):
            rolled = jnp.roll(bank, (row_shift, col_shift), axis=(1, 2)).reshape(bank.shape[0], -1)
            results.append(lax.dot_general(flat, rolled, (((1,), (1,)), ((), ())), preferred_element_type=jnp.float32))
    return jnp.stack(results, 2)

def reference(micrograph, templates, ref_bank, peak_offsets, peak_template, owners):
    cosine, sine = tables(L)
    normalized = normalize(templates)
    spectra = lax.map(lambda one: spectrum(one, cosine, sine), normalized)
    tiles = micrograph.reshape(N_BLK, L, N_GROUP, L).transpose(0, 2, 1, 3).reshape(N_BLK * N_GROUP, L, L)

    def search(tile):
        tile_spec = spectrum(tile, cosine, sine)

        def step(stats, tmpl_spec):
            return (accumulate(stats, correlate(tile_spec, tmpl_spec, cosine, sine)), None)
        init = (jnp.full((L, L), -jnp.inf, jnp.float32), jnp.zeros((L, L), jnp.float32), jnp.zeros((L, L), jnp.float32))
        stats, unused = lax.scan(step, init, spectra)
        return finish(stats, TEMPLATES)
    mip_tiles, z_tiles = lax.map(search, tiles)
    mip = mip_tiles.reshape(N_BLK, N_GROUP, L, L).transpose(0, 2, 1, 3).reshape(N_BLK * L, N_GROUP * L)
    zmap = z_tiles.reshape(N_BLK, N_GROUP, L, L).transpose(0, 2, 1, 3).reshape(N_BLK * L, N_GROUP * L)

    def refine(item):
        index, offsets, choice_slot, owner = item
        device = index // CANDS_DEV
        row_blk = device // N_GROUP
        col_group = device % N_GROUP
        tile = lax.dynamic_slice(micrograph, ((row_blk * L).astype(jnp.int32), (col_group * L).astype(jnp.int32)), (L, L))
        patch = cut_patch(tile, offsets)
        which = (owner * REF_DEV + choice_slot).astype(jnp.int32)
        bank = lax.dynamic_slice_in_dim(ref_bank, which, 1, 0)
        return score_shifts(patch.reshape(1, -1), bank)[0, 0]
    indices = jnp.arange(CANDIDATES, dtype=jnp.int32)
    refined = lax.map(refine, (indices, peak_offsets, peak_template, owners[:, 0]))
    return (mip, zmap, refined)
```

```python
import math

import jax
import jax.numpy as jnp
import numpy as np
from jax import lax
from jax.experimental import pallas as pl
from jax.experimental.pallas import tpu as pltpu
from jax.sharding import Mesh
from jax.sharding import PartitionSpec as P

L = 384
H = 192
Q = 96
SLABS = 64
ROWS = 40
WIDE = 1280
BF = jnp.bfloat16
F32 = jnp.float32
MB = 1024 * 1024
ROWS_OF = ("zl", "y")
COLS_OF = ("x", "zh", "core")
CHIPS = ("zl", "y", "x", "zh")


def dot(a, b):
    return jnp.dot(a, b, preferred_element_type=F32)


def wave(a, b):
    angle = (np.multiply.outer(np.asarray(a), np.asarray(b)) % L) * (2.0 * math.pi / L)
    return np.cos(angle), np.sin(angle)


def bf(a):
    return np.asarray(a, np.float32).astype(jnp.bfloat16)


def make_tables():
    n = np.arange(L)
    cos, sin = wave(n, n)
    forward = np.concatenate([cos[:H], cos[H : H + 1], sin[1:H]], 0)
    halves = np.stack(
        [np.concatenate([forward[c * Q : c * Q + Q], forward[H + c * Q : H + c * Q + Q]], 0) for c in range(2)]
    )
    pair = np.concatenate([cos, sin], 1)
    inverse_cols = np.concatenate([pair, np.concatenate([-sin, cos], 1)], 0)
    weight = np.full((H,), 2.0)
    weight[0] = 1.0
    inverse_rows = np.concatenate([cos[:, :H] * weight, -2.0 * sin[:, :H]], 1)
    inverse_rows[:, H] = cos[:, H]
    reverse = np.zeros((L, L))
    reverse[(-n) % L, n] = 1.0
    pick = np.zeros((4, L, 128))
    for part in range(4):
        pick[part, n, 80 + 6 * part + n % 6] = 1.0
    lane = np.arange(128)
    ac = lane % 16
    live = (ac < 9).astype(np.float64)
    a, c = ac // 3 - 1, ac % 3 - 1
    col_cos, col_sin = wave(n, c)
    turn = np.zeros((SLABS, 16, L))
    shift = np.zeros((SLABS, 8, 128))
    extra = np.zeros((SLABS, 16, 128))
    for s in range(SLABS):
        for part in range(3):
            k = s + 64 * part
            kc, ks = wave([k], n)
            turn[s, part], turn[s, 3 + part] = kc[0], ks[0]
            ac_, as_ = wave([k], a)
            w = (1.0 if k == 0 else 2.0) * live
            shift[s, part], shift[s, 3 + part] = ac_[0] * w, as_[0] * w
        turn[s, 6] = cos[H]
        sign = np.where(a == 0, 1.0, -1.0) * live
        extra[s, :6] = sign * col_cos[6 * s : 6 * s + 6]
        extra[s, 8:14] = -sign * col_sin[6 * s : 6 * s + 6]
    return dict(
        forward=bf(forward),
        halves=bf(halves),
        pair=bf(pair),
        inverse_cols=bf(inverse_cols),
        inverse_rows=bf(inverse_rows),
        reverse=bf(reverse),
        pick=bf(pick.reshape(4 * L, 128)),
        col_cos=col_cos.astype(np.float32),
        col_sin=col_sin.astype(np.float32),
        turn=bf(turn),
        shift=shift.astype(np.float32),
        extra=extra.astype(np.float32),
    )


TAB = make_tables()


def full_spec(shape):
    zeros = (0,) * len(shape)
    return pl.BlockSpec(shape, lambda i, ids: zeros)


def iota(shape, dim):
    return lax.broadcasted_iota(jnp.int32, shape, dim)


def spectra_kernel(ids, tile, ref, meta, forward, pair, pick, msg, spec, flat):
    rows64 = iota((SLABS, L), 0)
    owned = (iota((SLABS, L), 1) // 6) == rows64
    first_row = rows64 == 0
    flat[...] = jnp.zeros_like(flat)
    lasts = []
    for which, image in enumerate((tile[...], ref[0])):
        first = dot(forward[...], image).astype(BF)
        second = dot(first, pair[...])
        real = second[:H, :L] - second[H:, L:]
        imag = -(second[:H, L:] + second[H:, :L])
        if which == 0:
            spec[0] = real.astype(BF)
            spec[1] = imag.astype(BF)
        for plane, (full, alone) in enumerate(((real, second[:64, :L]), (imag, -second[:64, L:]))):
            for part in range(3):
                block = full[64 * part : 64 * part + 64]
                if part == 0:
                    block = jnp.where(first_row, alone, block)
                for j in range(3):
                    row = 18 * which + 9 * plane + 3 * part + j
                    flat[pl.ds(row, SLABS, stride=ROWS), :] = block[:, 128 * j : 128 * j + 128]
        for last in (second[H : H + 1, :L], -second[H : H + 1, L:]):
            lasts.append(jnp.where(owned, jnp.broadcast_to(last, (SLABS, L)), 0.0).astype(BF))
    line = dot(jnp.concatenate(lasts, 1), pick[...])
    flat[pl.ds(36, SLABS, stride=ROWS), :] = line + meta[...]
    msg[...] = flat[...].reshape(SLABS, ROWS, 128).astype(BF)


def make_spectra(ids, tile, bank, meta):
    return pl.pallas_call(
        spectra_kernel,
        out_shape=(
            jax.ShapeDtypeStruct((SLABS, ROWS, 128), BF),
            jax.ShapeDtypeStruct((2, H, L), BF),
        ),
        grid_spec=pltpu.PrefetchScalarGridSpec(
            num_scalar_prefetch=1,
            grid=(1,),
            in_specs=[
                full_spec((L, L)),
                pl.BlockSpec((1, L, L), lambda i, ids: (ids[0], 0, 0)),
                full_spec((1, 128)),
                full_spec((L, L)),
                full_spec((L, 2 * L)),
                full_spec((4 * L, 128)),
            ],
            out_specs=[full_spec((SLABS, ROWS, 128)), full_spec((2, H, L))],
            scratch_shapes=[pltpu.VMEM((SLABS * ROWS, 128), F32)],
        ),
        compiler_params=pltpu.CompilerParams(vmem_limit_bytes=40 * MB),
        cost_estimate=pl.CostEstimate(flops=800_000_000, bytes_accessed=3 * MB, transcendentals=0),
        name="tile_spectra",
    )(ids, tile, bank, meta, TAB["forward"], TAB["pair"], TAB["pick"])


def template_kernel(ids, template, halves, pair, half):
    values = template[0].astype(F32)
    count = 1.0 / (L * L)
    centre = jnp.sum(values) * count
    spread = values - centre
    power = jnp.sum(spread * spread) * count
    scale = 1.0 / (L * jnp.sqrt(jnp.full((1, 1), power + 1e-06, F32)))
    normalized = (spread * scale).astype(BF)
    first = dot(halves[0], normalized).astype(BF)
    second = dot(first, pair[...])
    half[0] = (second[:Q, :L] - second[Q:, L:]).astype(BF)
    half[1] = (-(second[:Q, L:] + second[Q:, :L])).astype(BF)


def template_half(ids, templates):
    return pl.pallas_call(
        template_kernel,
        out_shape=jax.ShapeDtypeStruct((2, Q, L), BF),
        grid_spec=pltpu.PrefetchScalarGridSpec(
            num_scalar_prefetch=1,
            grid=(1,),
            in_specs=[
                full_spec((1, L, L)),
                pl.BlockSpec((1, H, L), lambda i, ids: (ids[1], 0, 0)),
                full_spec((L, 2 * L)),
            ],
            out_specs=full_spec((2, Q, L)),
        ),
        compiler_params=pltpu.CompilerParams(vmem_limit_bytes=40 * MB),
        cost_estimate=pl.CostEstimate(flops=200_000_000, bytes_accessed=2 * MB, transcendentals=0),
        name="template_spectrum",
    )(ids, templates, TAB["halves"], TAB["pair"])


def refine_kernel(
    ids, own, other, pair, turn, shift, extra, col_cos, col_sin, out, flat, tiles, refs, waves, comb
):
    slab = ids[2]
    lane64 = iota((SLABS, 128), 1)

    def spread(base, target, rows):
        for plane in range(2):
            for j in range(9):
                col = plane * WIDE + 128 * j
                target[rows, col : col + 128] = flat[
                    pl.ds(base + 9 * plane + j, SLABS, stride=ROWS), :
                ].astype(target.dtype)
        line = flat[pl.ds(36, SLABS, stride=ROWS), :]
        for plane in range(2):
            at = 80 + (12 if base else 0) + 6 * plane
            moved = jnp.where(lane64 < 6, pltpu.roll(line, 128 - at, axis=1), 0.0)
            col = plane * WIDE + 1152
            target[rows, col : col + 128] = moved.astype(target.dtype)
        return line

    flat[...] = other[...].astype(F32).reshape(SLABS * ROWS, 128)
    spread(18, refs, slice(64, 128))
    flat[...] = own[...].astype(F32).reshape(SLABS * ROWS, 128)
    spread(18, refs, slice(0, 64))
    meta = spread(0, tiles, slice(0, 64)).astype(BF)

    waves[:, : 2 * L] = pair[...]
    wanted = (iota((L, 128), 0) == iota((L, 128), 1) + 6 * slab).astype(BF)
    waves[:, 768:896] = dot(pair[:, :L], wanted).astype(BF)
    waves[:, 896:1024] = dot(pair[:, L:], wanted).astype(BF)

    for part in range(3):
        cos_a, sin_a = shift[0, part : part + 1], shift[0, 3 + part : 4 + part]
        rows = slice(L * part, L * part + L)
        comb[rows] = (cos_a * col_cos[...] - sin_a * col_sin[...]).astype(BF)
        rows = slice(WIDE + L * part, WIDE + L * part + L)
        comb[rows] = (-(sin_a * col_cos[...] + cos_a * col_sin[...])).astype(BF)
    pad = jnp.zeros((112, 128), F32)
    tail = jnp.zeros((8, 128), F32)
    comb[1152:1280] = jnp.concatenate([extra[0, :8], tail, pad], 0).astype(BF)
    comb[WIDE + 1152 : WIDE + 1280] = jnp.concatenate([extra[0, 8:], tail, pad], 0).astype(BF)

    row = iota((128, 128), 0)
    lane = iota((128, 128), 1)
    mine = (lane % 16) == (row % 16)
    field = lane // 16
    place = jnp.where(mine, 1.0, 0.0)
    w_x = jnp.where(field == 0, 128.0, jnp.where(field == 1, 1.0, 0.0)) * place
    w_y = jnp.where(field == 2, 128.0, jnp.where(field == 3, 1.0, 0.0)) * place
    w_t = jnp.where(field == 4, 1.0, 0.0) * place
    kept = (lane // 16) == (row % 8)
    lane_l = iota((128, L), 1).astype(F32)
    lane_t = lane.astype(F32)

    def chunk(q, carry):
        repeat = (iota((128, SLABS), 1) == 8 * q + iota((128, SLABS), 0) // 16).astype(BF)
        fields = dot(repeat, meta)
        ox = jnp.sum(fields * w_x, axis=1, keepdims=True)
        oy = jnp.sum(fields * w_y, axis=1, keepdims=True)
        choice = jnp.sum(fields * w_t, axis=1, keepdims=True)
        ref = dot((lane_t == choice).astype(BF), refs[...])
        wave_y = dot((lane_l == oy).astype(BF), waves[...])
        wave_x = lax.dot_general(
            (lane_l == ox).astype(BF), turn[0], (((1,), (1,)), ((), ())), preferred_element_type=F32
        )
        tile = tiles[pl.ds(pl.multiple_of(8 * q, 8), 8), :]
        total = jnp.zeros((128, 128), F32)
        for part in range(4):
            at = L * part
            size = L if part < 3 else 128
            tile_r = jnp.broadcast_to(tile[:, None, at : at + size], (8, 16, size)).reshape(128, size)
            tile_i = jnp.broadcast_to(
                tile[:, None, WIDE + at : WIDE + at + size], (8, 16, size)
            ).reshape(128, size)
            ref_r, ref_i = ref[:, at : at + size], ref[:, WIDE + at : WIDE + at + size]
            if part < 3:
                cos_y, sin_y = wave_y[:, :L], wave_y[:, L : 2 * L]
                cos_x, sin_x = wave_x[:, part : part + 1], wave_x[:, 3 + part : 4 + part]
                turn_r = cos_y * cos_x - sin_y * sin_x
                turn_i = sin_y * cos_x + cos_y * sin_x
            else:
                cos_x = wave_x[:, 6:7]
                turn_r = wave_y[:, 768:896] * cos_x
                turn_i = wave_y[:, 896:1024] * cos_x
            prod_r = tile_r * ref_r + tile_i * ref_i
            prod_i = tile_i * ref_r - tile_r * ref_i
            both_r = (prod_r * turn_r - prod_i * turn_i).astype(BF)
            both_i = (prod_r * turn_i + prod_i * turn_r).astype(BF)
            total += dot(both_r, comb[at : at + size])
            total += dot(both_i, comb[WIDE + at : WIDE + at + size])
        total = jnp.where(kept, total * (1.0 / (L * L)), 0.0)
        out[pl.ds(pl.multiple_of(16 * q, 16), 16), :] = jnp.sum(total.reshape(16, 8, 128), axis=1)
        return carry

    lax.fori_loop(0, 8, chunk, 0)


def refine(ids, own, other):
    by_slab = lambda i, ids: (ids[2], 0, 0)
    return pl.pallas_call(
        refine_kernel,
        out_shape=jax.ShapeDtypeStruct((128, 128), F32),
        grid_spec=pltpu.PrefetchScalarGridSpec(
            num_scalar_prefetch=1,
            grid=(1,),
            in_specs=[
                full_spec((SLABS, ROWS, 128)),
                full_spec((SLABS, ROWS, 128)),
                full_spec((L, 2 * L)),
                pl.BlockSpec((1, 16, L), by_slab),
                pl.BlockSpec((1, 8, 128), by_slab),
                pl.BlockSpec((1, 16, 128), by_slab),
                full_spec((L, 128)),
                full_spec((L, 128)),
            ],
            out_specs=full_spec((128, 128)),
            scratch_shapes=[
                pltpu.VMEM((SLABS * ROWS, 128), F32),
                pltpu.VMEM((SLABS, 2 * WIDE), F32),
                pltpu.VMEM((128, 2 * WIDE), BF),
                pltpu.VMEM((L, 1024), BF),
                pltpu.VMEM((2 * WIDE, 128), BF),
            ],
        ),
        compiler_params=pltpu.CompilerParams(vmem_limit_bytes=48 * MB),
        cost_estimate=pl.CostEstimate(flops=4_000_000_000, bytes_accessed=3 * MB, transcendentals=0),
        name="refine_slab",
    )(
        ids, own, other, TAB["pair"], TAB["turn"], TAB["shift"], TAB["extra"], TAB["col_cos"], TAB["col_sin"]
    )


def search_kernel(ids, spec, o0, o1, o2, o3, p0, p1, p2, p3, cols, rows, reverse, mip, zmap, prod, total, square):
    core = ids[1]
    mine = pl.ds(pl.multiple_of(core * Q, Q), Q)
    yours = pl.ds(pl.multiple_of((1 - core) * Q, Q), Q)
    index = [(own, oth, z) for own, oth in ((o0, p0), (o1, p1), (o2, p2), (o3, p3)) for z in range(2)]
    row16 = iota((16, L), 0)
    zero = jnp.zeros((16, L), F32)
    ends_r, ends_i = zero, zero
    for n, (own, oth, z) in enumerate(index):
        for ref, where in ((own, mine), (oth, yours)):
            tile_r, tile_i = spec[0, where, :].astype(F32), spec[1, where, :].astype(F32)
            t_r, t_i = ref[z, 0].astype(F32), ref[z, 1].astype(F32)
            prod[n, where, :L] = (tile_r * t_r + tile_i * t_i).astype(BF)
            prod[n, where, L:] = (tile_i * t_r - tile_r * t_i).astype(BF)
        top_r = jnp.where(core == 0, own[z, 0, :16].astype(F32), oth[z, 0, :16].astype(F32))
        top_i = jnp.where(core == 0, own[z, 1, :16].astype(F32), oth[z, 1, :16].astype(F32))
        ends_r = jnp.where(row16 == n, top_r[0:1], ends_r)
        ends_i = jnp.where(row16 == n, top_i[0:1], ends_i)
    ends_r = jnp.where(row16 == 8, spec[0, :16].astype(F32)[0:1], ends_r)
    ends_i = jnp.where(row16 == 8, spec[1, :16].astype(F32)[0:1], ends_i)
    back_r = dot(ends_r.astype(BF), reverse[...])
    back_i = dot(ends_i.astype(BF), reverse[...])
    low_r, low_i = 0.5 * (ends_r + back_r), 0.5 * (ends_i - back_i)
    top_r, top_i = -0.5 * (ends_i + back_i), 0.5 * (ends_r - back_r)

    def cross(a_r, a_i):
        s_r, s_i = a_r[8:9], a_i[8:9]
        return s_r * a_r + s_i * a_i, s_i * a_r - s_r * a_i

    low = cross(low_r, low_i)
    top = cross(top_r, top_i)
    line_r = low[0] - top[1]
    line_i = low[1] + top[0]
    for n in range(8):
        for at, line in ((0, line_r), (L, line_i)):
            old = prod[n, :16, at : at + L].astype(F32)
            prod[n, :16, at : at + L] = jnp.where(row16 == 0, line[n : n + 1], old).astype(BF)

    def step(pair, carry):
        both = []
        for k in range(2):
            middle = dot(prod[2 * pair + k], cols[...]).astype(BF)
            both.append(jnp.concatenate([middle[:, :L], middle[:, L:]], 0))
        corr = dot(rows[...], jnp.concatenate(both, 1)) * (1.0 / (L * L))
        one, two = corr[:, :L], corr[:, L:]
        largest = jnp.maximum(one, two)
        summed = one + two
        powers = one * one + two * two

        @pl.when(pair == 0)
        def _():
            mip[...] = largest
            total[...] = summed
            square[...] = powers

        @pl.when(pair > 0)
        def _():
            mip[...] = jnp.maximum(mip[...], largest)
            total[...] += summed
            square[...] += powers

        return carry

    lax.fori_loop(0, 4, step, 0)
    mean = total[...] * 0.125
    var = square[...] * 0.125 - mean * mean
    zmap[...] = (mip[...] - mean) * lax.rsqrt(jnp.maximum(var, 0.25))


def search(ids, spec, owns, others):
    piece = full_spec((2, 2, Q, L))
    return pl.pallas_call(
        search_kernel,
        out_shape=(jax.ShapeDtypeStruct((L, L), F32), jax.ShapeDtypeStruct((L, L), F32)),
        grid_spec=pltpu.PrefetchScalarGridSpec(
            num_scalar_prefetch=1,
            grid=(1,),
            in_specs=[full_spec((2, H, L))]
            + [piece] * 8
            + [full_spec((2 * L, 2 * L)), full_spec((L, L)), full_spec((L, L))],
            out_specs=[full_spec((L, L)), full_spec((L, L))],
            scratch_shapes=[
                pltpu.VMEM((8, H, 2 * L), BF),
                pltpu.VMEM((L, L), F32),
                pltpu.VMEM((L, L), F32),
            ],
        ),
        compiler_params=pltpu.CompilerParams(vmem_limit_bytes=48 * MB),
        cost_estimate=pl.CostEstimate(flops=4_000_000_000, bytes_accessed=6 * MB, transcendentals=0),
        name="search_templates",
    )(ids, spec, *owns, *others, TAB["inverse_cols"], TAB["inverse_rows"], TAB["reverse"])


def ring(count, step):
    return [(i, (i + step) % count) for i in range(count)]


def body(micrograph, templates, ref_bank, peak_offsets, peak_template, owners):
    blk = lax.axis_index(ROWS_OF)
    group = lax.axis_index(COLS_OF)
    core = lax.axis_index("core")
    ids = jnp.stack([blk, core, blk * 8 + group // 2]).astype(jnp.int32)
    owner = owners[:, 0]
    choice = peak_template * 8 + owner // 2 + 64 * ((owner % 2) ^ core)
    ox, oy = peak_offsets[:, 0], peak_offsets[:, 1]
    meta = jnp.concatenate([ox // 128, ox % 128, oy // 128, oy % 128, choice, jnp.zeros((48,), jnp.int32)])
    meta = meta.astype(F32).reshape(1, 128)

    def across(array):
        return lax.ppermute(array, "core", ring(2, 1))

    message, spec = make_spectra(ids, micrograph, ref_bank, meta)
    arrived = lax.all_to_all(message, CHIPS, 0, 0, tiled=True)
    half = template_half(ids, templates)
    near = lax.ppermute(half, "zl", ring(2, 1))
    both = jnp.stack([half, near])
    owns = [both] + [lax.ppermute(both, "y", ring(4, step)) for step in (1, 3, 2)]
    others = [across(one) for one in owns]
    scores = refine(ids, arrived, across(arrived))
    returned = lax.all_to_all(scores.reshape(SLABS, 2, 128), CHIPS, 0, 0, tiled=True)
    mip, zmap = search(ids, spec, owns, others)
    refined = jnp.sum(returned, 0).reshape(16, 16)[:, :9]
    return (mip, zmap, refined)


def solution(mesh):
    inner = Mesh(mesh.devices.reshape(2, 4, 4, 2, 2), ("zl", "y", "x", "zh", "core"))
    every = ROWS_OF + COLS_OF
    placed = (
        P(ROWS_OF, COLS_OF),
        P(ROWS_OF, None, None),
        P(COLS_OF, None, None),
        P(every, None),
        P(every),
        P(every, None),
    )
    return jax.shard_map(
        body,
        mesh=inner,
        in_specs=placed,
        out_specs=(P(ROWS_OF, COLS_OF), P(ROWS_OF, COLS_OF), P(every, None)),
        check_vma=False,
    )
```

```python
import math

import jax
import jax.numpy as jnp
import numpy as np
from jax import lax
from jax.experimental import pallas as pl
from jax.experimental.pallas import tpu as pltpu
from jax.sharding import Mesh
from jax.sharding import PartitionSpec as P

L = 384
H = 192
Q = 96
SLABS = 64
ROWS = 40
WIDE = 1280
BF = jnp.bfloat16
F32 = jnp.float32
MB = 1024 * 1024
ROWS_OF = ("zl", "y")
COLS_OF = ("x", "zh", "core")
CHIPS = ("zl", "y", "x", "zh")


def dot(a, b):
    return jnp.dot(a, b, preferred_element_type=F32)


def wave(a, b):
    angle = (np.multiply.outer(np.asarray(a), np.asarray(b)) % L) * (2.0 * math.pi / L)
    return np.cos(angle), np.sin(angle)


def bf(a):
    return np.asarray(a, np.float32).astype(jnp.bfloat16)


def make_tables():
    n = np.arange(L)
    cos, sin = wave(n, n)
    forward = np.concatenate([cos[:H], cos[H : H + 1], sin[1:H]], 0)
    halves = np.stack(
        [np.concatenate([forward[c * Q : c * Q + Q], forward[H + c * Q : H + c * Q + Q]], 0) for c in range(2)]
    )
    pair = np.concatenate([cos, sin], 1)
    inverse_cols = np.concatenate([pair, np.concatenate([-sin, cos], 1)], 0)
    weight = np.full((H,), 2.0)
    weight[0] = 1.0
    inverse_rows = np.concatenate([cos[:, :H] * weight, -2.0 * sin[:, :H]], 1)
    inverse_rows[:, H] = cos[:, H]
    reverse = np.zeros((L, L))
    reverse[(-n) % L, n] = 1.0
    pick = np.zeros((4, L, 128))
    for part in range(4):
        pick[part, n, 80 + 6 * part + n % 6] = 1.0
    lane = np.arange(128)
    field = np.zeros((128, 3, 128))
    for which, at in enumerate((0, 32, 64)):
        if which < 2:
            field[at : at + 16, which] = 128.0
            at += 16
        field[at : at + 16, which] = 1.0
    ac = lane % 16
    a, c = ac // 3 - 1, ac % 3 - 1
    comb = np.zeros((2, 3, L, 128))
    extra = np.zeros((SLABS, 2, 8, 128))
    for shift in (-1, 0, 1):
        kc, ks = wave(n, [shift])
        for part in range(4):
            at = 6 * part + 2 * (shift + 1)
            if part < 3:
                comb[0, part, :, at], comb[0, part, :, at + 1] = kc[:, 0], ks[:, 0]
                comb[1, part, :, at], comb[1, part, :, at + 1] = -ks[:, 0], kc[:, 0]
            else:
                kc, ks = kc[:, 0].reshape(SLABS, 6), ks[:, 0].reshape(SLABS, 6)
                extra[:, 0, :6, at], extra[:, 0, :6, at + 1] = kc, ks
                extra[:, 1, :6, at], extra[:, 1, :6, at + 1] = -ks, kc
    turn = np.zeros((SLABS, 16, L))
    widen = np.zeros((256, 16))
    last = np.zeros((SLABS, 2, 128, 128))
    for part in range(4):
        widen[6 * part : 6 * part + 6, part] = 1.0
        widen[128 + 6 * part : 128 + 6 * part + 6, 4 + part] = 1.0
    for s in range(SLABS):
        for part in range(4):
            k = s + 64 * part if part < 3 else H
            kc, ks = wave([k], n)
            turn[s, part], turn[s, 4 + part] = kc[0], ks[0]
            ca, sa = wave([k], a)
            w = 1.0 if k in (0, H) else 2.0
            for shift in (-1, 0, 1):
                at = 6 * part + 2 * (shift + 1)
                on = w * ((ac < 9) & (c == shift))
                last[s, 0, at], last[s, 0, at + 1] = on * ca[0], -on * sa[0]
                last[s, 1, at], last[s, 1, at + 1] = -on * sa[0], -on * ca[0]
    return dict(
        forward=bf(forward),
        halves=bf(halves),
        pair=bf(pair),
        inverse_cols=bf(inverse_cols),
        inverse_rows=bf(inverse_rows),
        reverse=bf(reverse),
        pick=bf(pick.reshape(4 * L, 128)),
        field=bf(field.reshape(128, 384)),
        comb=bf(comb.reshape(6 * L, 128)),
        extra=bf(extra.reshape(SLABS, 16, 128)),
        turn=bf(turn),
        widen=bf(widen),
        last=bf(last.reshape(SLABS, 256, 128)),
    )


TAB = make_tables()


def full_spec(shape):
    zeros = (0,) * len(shape)
    return pl.BlockSpec(shape, lambda i, ids: zeros)


def iota(shape, dim):
    return lax.broadcasted_iota(jnp.int32, shape, dim)


def prepare_kernel(
    ids,
    offsets,
    choice,
    owners,
    tile_hbm,
    template_hbm,
    bank_hbm,
    forward_hbm,
    pair_hbm,
    halves_hbm,
    pick_hbm,
    msg,
    spec,
    half,
    flat,
    tile,
    template,
    ref,
    forward,
    pair,
    rows_half,
    pick,
    sems,
):
    blk, core = ids[0], ids[1]
    jobs = (
        (forward_hbm, forward),
        (tile_hbm, tile),
        (pair_hbm, pair),
        (bank_hbm.at[blk], ref),
        (pick_hbm, pick),
        (template_hbm.at[0], template),
        (halves_hbm.at[core], rows_half),
    )
    copies = [pltpu.make_async_copy(src, dst, sems.at[n]) for n, (src, dst) in enumerate(jobs)]
    for copy in copies:
        copy.start()

    r8 = iota((8, 16), 0)
    ox, oy = offsets[0:1], offsets[1:2]
    owner = owners[...]
    named = choice[...] * 8 + (owner >> 1) + 64 * ((owner & 1) ^ core)
    values = jnp.where(r8 == 4, named, 0)
    for n, value in enumerate((ox >> 7, ox & 127, oy >> 7, oy & 127)):
        values = jnp.where(r8 == n, value, values)
    wide = ((iota((16, 128), 1) & 15) == iota((16, 128), 0)).astype(BF)
    lined = dot(values.astype(F32).astype(BF), wide)
    lined = jnp.where((iota((8, 128), 1) >> 4) == iota((8, 128), 0), lined, 0.0)
    meta = jnp.sum(lined, axis=0, keepdims=True)

    rows64 = iota((SLABS, L), 0)
    owned = (iota((SLABS, L), 1) // 6) == rows64
    first_row = rows64 == 0
    for row in range(37, ROWS):
        flat[pl.ds(row, SLABS, stride=ROWS), :] = jnp.zeros((SLABS, 128), F32)
    copies[0].wait()
    lasts = []
    for which, image in enumerate((tile, ref)):
        copies[1 + 2 * which].wait()
        first = dot(forward[...], image[...]).astype(BF)
        if which == 0:
            copies[2].wait()
        second = dot(first, pair[...])
        real = second[:H, :L] - second[H:, L:]
        imag = -(second[:H, L:] + second[H:, :L])
        if which == 0:
            spec[0] = real.astype(BF)
            spec[1] = imag.astype(BF)
        for plane, (full, alone) in enumerate(((real, second[:64, :L]), (imag, -second[:64, L:]))):
            for part in range(3):
                block = full[64 * part : 64 * part + 64]
                if part == 0:
                    block = jnp.where(first_row, alone, block)
                for j in range(3):
                    row = 18 * which + 9 * plane + 3 * part + j
                    flat[pl.ds(row, SLABS, stride=ROWS), :] = block[:, 128 * j : 128 * j + 128]
        for last in (second[H : H + 1, :L], -second[H : H + 1, L:]):
            lasts.append(jnp.where(owned, jnp.broadcast_to(last, (SLABS, L)), 0.0).astype(BF))
    copies[4].wait()
    line = dot(jnp.concatenate(lasts, 1), pick[...])
    flat[pl.ds(36, SLABS, stride=ROWS), :] = line + meta
    msg[...] = flat[...].reshape(SLABS, ROWS, 128).astype(BF)

    copies[5].wait()
    copies[6].wait()
    values = template[...].astype(F32)
    count = 1.0 / (L * L)
    spread = values - jnp.sum(values) * count
    power = jnp.sum(spread * spread) * count
    scale = 1.0 / (L * jnp.sqrt(jnp.full((1, 1), power + 1e-06, F32)))
    normalized = (spread * scale).astype(BF)
    first = dot(rows_half[...], normalized).astype(BF)
    second = dot(first, pair[...])
    real = (second[:Q, :L] - second[Q:, L:]).astype(BF)
    imag = (-(second[:Q, L:] + second[Q:, :L])).astype(BF)
    for n in range(8):
        half[n, 0] = real
        half[n, 1] = imag


def prepare(ids, offsets, choice, owners, tile, templates, bank):
    held = pl.BlockSpec(memory_space=pltpu.HBM)
    return pl.pallas_call(
        prepare_kernel,
        out_shape=(
            jax.ShapeDtypeStruct((SLABS, ROWS, 128), BF),
            jax.ShapeDtypeStruct((2, H, L), BF),
            jax.ShapeDtypeStruct((8, 2, Q, L), BF),
        ),
        grid_spec=pltpu.PrefetchScalarGridSpec(
            num_scalar_prefetch=1,
            grid=(1,),
            in_specs=[full_spec((2, 16)), full_spec((1, 16)), full_spec((1, 16))] + [held] * 7,
            out_specs=[full_spec((SLABS, ROWS, 128)), full_spec((2, H, L)), full_spec((8, 2, Q, L))],
            scratch_shapes=[
                pltpu.VMEM((SLABS * ROWS, 128), F32),
                pltpu.VMEM((L, L), BF),
                pltpu.VMEM((L, L), BF),
                pltpu.VMEM((L, L), BF),
                pltpu.VMEM((L, L), BF),
                pltpu.VMEM((L, 2 * L), BF),
                pltpu.VMEM((H, L), BF),
                pltpu.VMEM((4 * L, 128), BF),
                pltpu.SemaphoreType.DMA((7,)),
            ],
        ),
        compiler_params=pltpu.CompilerParams(vmem_limit_bytes=62 * MB),
        cost_estimate=pl.CostEstimate(flops=1_000_000_000, bytes_accessed=4 * MB, transcendentals=0),
        name="prepare_spectra",
    )(
        ids, offsets, choice, owners, tile, templates, bank,
        TAB["forward"], TAB["pair"], TAB["halves"], TAB["pick"],
    )


MAIN = 6 * L
N_CAND = 1024


def refine_kernel(
    own, other, pair, field, comb, widen, turn, extra, last, slab_ref, out,
    flat, tiles, refs, waves, ref_of, wave_of, both, turned,
):
    slab = slab_ref[2]
    lane64 = iota((SLABS, 128), 1)

    def spread(base, target, rows):
        for col in range(18):
            target[rows, 128 * col : 128 * col + 128] = flat[pl.ds(base + col, SLABS, stride=ROWS), :].astype(
                target.dtype
            )
        line = flat[pl.ds(36, SLABS, stride=ROWS), :]
        for plane in range(2):
            at = 80 + (12 if base else 0) + 6 * plane
            moved = jnp.where(lane64 < 6, pltpu.roll(line, 128 - at, axis=1), 0.0)
            target[rows, MAIN + 128 * plane : MAIN + 128 * plane + 128] = moved.astype(target.dtype)
        return line

    flat[...] = other[...].astype(F32).reshape(SLABS * ROWS, 128)
    spread(18, refs, slice(64, 128))
    flat[...] = own[...].astype(F32).reshape(SLABS * ROWS, 128)
    spread(18, refs, slice(0, 64))
    meta = spread(0, tiles, slice(0, 64)).astype(BF)

    waves[:, : 2 * L] = pair[...]
    wanted = (iota((L, 128), 0) == iota((L, 128), 1) + 6 * slab).astype(BF)
    waves[:, 768:896] = dot(pair[:, :L], wanted).astype(BF)
    waves[:, 896:1024] = dot(pair[:, L:], wanted).astype(BF)
    turns = dot(widen[...], turn[0]).astype(BF)
    pad = jnp.zeros((112, 128), BF)
    ends = jnp.concatenate(
        [
            jnp.concatenate([extra[0, :8].astype(F32), jnp.zeros((8, 128), F32)], 0).astype(BF),
            pad,
            jnp.concatenate([extra[0, 8:].astype(F32), jnp.zeros((8, 128), F32)], 0).astype(BF),
            pad,
        ],
        0,
    )

    block = 256
    rowb = iota((block, 128), 0)
    laneb = iota((block, 128), 1)
    mine = (laneb & 15) == (rowb & 15)
    lanef = laneb.astype(F32)

    def gather(q, carry):
        rows = pl.ds(pl.multiple_of(block * q, block), block)
        repeat = iota((block, SLABS), 1) == 16 * q + (iota((block, SLABS), 0) >> 4)
        fields = dot(repeat.astype(BF), meta)
        spots = dot(jnp.where(mine, fields, 0.0).astype(BF), field[...])
        hot_x = jnp.concatenate([(lanef + 128.0 * j == spots[:, :128]).astype(BF) for j in range(3)], 1)
        hot_y = jnp.concatenate([(lanef + 128.0 * j == spots[:, 128:256]).astype(BF) for j in range(3)], 1)
        hot_t = (lanef == spots[:, 256:]).astype(BF)
        ref_of[rows, :] = dot(hot_t, refs[...]).astype(BF)
        wave_of[rows, :] = dot(hot_y, waves[...]).astype(BF)
        turned[rows, :] = lax.dot_general(
            hot_x, turns, (((1,), (1,)), ((), ())), preferred_element_type=F32
        ).astype(BF)
        return carry

    lax.fori_loop(0, N_CAND // block, gather, 0)

    def multiply(q, carry):
        eight = pl.ds(pl.multiple_of(8 * q, 8), 8)
        for size, wave_at, places in (
            (L, 0, tuple((L * part, 3 * L + L * part) for part in range(3))),
            (128, 2 * L, ((MAIN, MAIN + 128),)),
        ):
            for at_r, at_i in places:
                tiles_r = tiles[eight, at_r : at_r + size]
                tiles_i = tiles[eight, at_i : at_i + size]
                for j in range(8):
                    rows = pl.ds(pl.multiple_of(128 * q + 16 * j, 16), 16)
                    cos_y = wave_of[rows, wave_at : wave_at + size].astype(F32)
                    sin_y = wave_of[rows, wave_at + size : wave_at + 2 * size].astype(F32)
                    tile_r, tile_i = tiles_r[j : j + 1], tiles_i[j : j + 1]
                    ref_r = ref_of[rows, at_r : at_r + size].astype(F32)
                    ref_i = ref_of[rows, at_i : at_i + size].astype(F32)
                    prod_r = tile_r * ref_r + tile_i * ref_i
                    prod_i = tile_i * ref_r - tile_r * ref_i
                    both[rows, at_r : at_r + size] = (prod_r * cos_y - prod_i * sin_y).astype(BF)
                    both[rows, at_i : at_i + size] = (prod_r * sin_y + prod_i * cos_y).astype(BF)
        return carry

    lax.fori_loop(0, 8, multiply, 0)

    kept = (laneb >> 4) == (rowb & 7)

    def finish(q, carry):
        rows = pl.ds(pl.multiple_of(block * q, block), block)
        sums = dot(both[rows, :MAIN], comb[...]) + dot(both[rows, MAIN:], ends)
        kappa = turned[rows, :].astype(F32)
        mixed = jnp.concatenate([(sums * kappa[:, :128]).astype(BF), (sums * kappa[:, 128:]).astype(BF)], 1)
        total = jnp.where(kept, dot(mixed, last[0]) * (1.0 / (L * L)), 0.0)
        to = pl.ds(pl.multiple_of(block // 8 * q, block // 8), block // 8)
        out[to, :] = jnp.sum(total.reshape(block // 8, 8, 128), axis=1)
        return carry

    lax.fori_loop(0, N_CAND // block, finish, 0)


def refine(ids, own, other):
    by_slab = lambda i, ids: (ids[2], 0, 0)

    def kernel(ids_ref, *refs):
        refine_kernel(*refs[:9], ids_ref, *refs[9:])

    return pl.pallas_call(
        kernel,
        out_shape=jax.ShapeDtypeStruct((128, 128), F32),
        grid_spec=pltpu.PrefetchScalarGridSpec(
            num_scalar_prefetch=1,
            grid=(1,),
            in_specs=[
                full_spec((SLABS, ROWS, 128)),
                full_spec((SLABS, ROWS, 128)),
                full_spec((L, 2 * L)),
                full_spec((128, 384)),
                full_spec((MAIN, 128)),
                full_spec((256, 16)),
                pl.BlockSpec((1, 16, L), by_slab),
                pl.BlockSpec((1, 16, 128), by_slab),
                pl.BlockSpec((1, 256, 128), by_slab),
            ],
            out_specs=full_spec((128, 128)),
            scratch_shapes=[
                pltpu.VMEM((SLABS * ROWS, 128), F32),
                pltpu.VMEM((SLABS, MAIN + 256), F32),
                pltpu.VMEM((128, MAIN + 256), BF),
                pltpu.VMEM((L, 1024), BF),
                pltpu.VMEM((N_CAND, MAIN + 256), BF),
                pltpu.VMEM((N_CAND, 1024), BF),
                pltpu.VMEM((N_CAND, MAIN + 256), BF),
                pltpu.VMEM((N_CAND, 256), BF),
            ],
        ),
        compiler_params=pltpu.CompilerParams(vmem_limit_bytes=62 * MB),
        cost_estimate=pl.CostEstimate(flops=6_000_000_000, bytes_accessed=4 * MB, transcendentals=0),
        name="refine_slab",
    )(
        ids, own, other, TAB["pair"], TAB["field"], TAB["comb"], TAB["widen"], TAB["turn"], TAB["extra"], TAB["last"]
    )


def search_kernel(ids, spec, own, oth, cols, rows, reverse, mip, zmap, prod, total, square):
    core = ids[1]
    mine = pl.ds(pl.multiple_of(core * Q, Q), Q)
    yours = pl.ds(pl.multiple_of((1 - core) * Q, Q), Q)
    row16 = iota((16, L), 0)
    zero = jnp.zeros((16, L), F32)
    ends_r, ends_i = zero, zero
    for n in range(8):
        for ref, where in ((own, mine), (oth, yours)):
            tile_r, tile_i = spec[0, where, :].astype(F32), spec[1, where, :].astype(F32)
            t_r, t_i = ref[n, 0].astype(F32), ref[n, 1].astype(F32)
            prod[n, where, :L] = (tile_r * t_r + tile_i * t_i).astype(BF)
            prod[n, where, L:] = (tile_i * t_r - tile_r * t_i).astype(BF)
        top_r = jnp.where(core == 0, own[n, 0, :16].astype(F32), oth[n, 0, :16].astype(F32))
        top_i = jnp.where(core == 0, own[n, 1, :16].astype(F32), oth[n, 1, :16].astype(F32))
        ends_r = jnp.where(row16 == n, top_r[0:1], ends_r)
        ends_i = jnp.where(row16 == n, top_i[0:1], ends_i)
    ends_r = jnp.where(row16 == 8, spec[0, :16].astype(F32)[0:1], ends_r)
    ends_i = jnp.where(row16 == 8, spec[1, :16].astype(F32)[0:1], ends_i)
    back_r = dot(ends_r.astype(BF), reverse[...])
    back_i = dot(ends_i.astype(BF), reverse[...])
    low_r, low_i = 0.5 * (ends_r + back_r), 0.5 * (ends_i - back_i)
    top_r, top_i = -0.5 * (ends_i + back_i), 0.5 * (ends_r - back_r)

    def cross(a_r, a_i):
        s_r, s_i = a_r[8:9], a_i[8:9]
        return s_r * a_r + s_i * a_i, s_i * a_r - s_r * a_i

    low = cross(low_r, low_i)
    top = cross(top_r, top_i)
    line_r = low[0] - top[1]
    line_i = low[1] + top[0]
    for n in range(8):
        for at, line in ((0, line_r), (L, line_i)):
            old = prod[n, :16, at : at + L].astype(F32)
            prod[n, :16, at : at + L] = jnp.where(row16 == 0, line[n : n + 1], old).astype(BF)

    def step(pair, carry):
        both = []
        stacked = prod[pl.ds(2 * pair, 2)].reshape(2 * H, 2 * L)
        middle = dot(stacked, cols[...]).astype(BF)
        for k in range(2):
            part = middle[H * k : H * k + H]
            both.append(jnp.concatenate([part[:, :L], part[:, L:]], 0))
        corr = dot(rows[...], jnp.concatenate(both, 1)) * (1.0 / (L * L))
        one, two = corr[:, :L], corr[:, L:]
        largest = jnp.maximum(one, two)
        summed = one + two
        powers = one * one + two * two

        @pl.when(pair == 0)
        def _():
            mip[...] = largest
            total[...] = summed
            square[...] = powers

        @pl.when(pair > 0)
        def _():
            mip[...] = jnp.maximum(mip[...], largest)
            total[...] += summed
            square[...] += powers

        return carry

    lax.fori_loop(0, 4, step, 0)
    mean = total[...] * 0.125
    var = square[...] * 0.125 - mean * mean
    zmap[...] = (mip[...] - mean) * lax.rsqrt(jnp.maximum(var, 0.25))


def search(ids, spec, own, other):
    piece = full_spec((8, 2, Q, L))
    return pl.pallas_call(
        search_kernel,
        out_shape=(jax.ShapeDtypeStruct((L, L), F32), jax.ShapeDtypeStruct((L, L), F32)),
        grid_spec=pltpu.PrefetchScalarGridSpec(
            num_scalar_prefetch=1,
            grid=(1,),
            in_specs=[full_spec((2, H, L))]
            + [piece] * 2
            + [full_spec((2 * L, 2 * L)), full_spec((L, L)), full_spec((L, L))],
            out_specs=[full_spec((L, L)), full_spec((L, L))],
            scratch_shapes=[
                pltpu.VMEM((8, H, 2 * L), BF),
                pltpu.VMEM((L, L), F32),
                pltpu.VMEM((L, L), F32),
            ],
        ),
        compiler_params=pltpu.CompilerParams(vmem_limit_bytes=62 * MB),
        cost_estimate=pl.CostEstimate(flops=4_000_000_000, bytes_accessed=6 * MB, transcendentals=0),
        name="search_templates",
    )(ids, spec, own, other, TAB["inverse_cols"], TAB["inverse_rows"], TAB["reverse"])


def ring(count, step):
    return [(i, (i + step) % count) for i in range(count)]


def body(micrograph, templates, ref_bank, peak_offsets, peak_template, owners):
    blk = lax.axis_index(ROWS_OF)
    group = lax.axis_index(COLS_OF)
    core = lax.axis_index("core")
    ids = jnp.stack([blk, core, blk * 8 + group // 2]).astype(jnp.int32)

    def across(array):
        return lax.ppermute(array, "core", ring(2, 1))

    message, spec, copies = prepare(
        ids,
        peak_offsets.T,
        peak_template.reshape(1, 16),
        owners.reshape(1, 16),
        micrograph,
        templates,
        ref_bank,
    )
    arrived = lax.all_to_all(message, CHIPS, 0, 0, tiled=True)
    arrived, copies = lax.optimization_barrier((arrived, copies))
    seen = lax.all_to_all(copies, ROWS_OF, 0, 0, tiled=True)
    scores = refine(ids, arrived, across(arrived))
    scores, seen = lax.optimization_barrier((scores, seen))
    returned = lax.all_to_all(scores.reshape(SLABS, 2, 128), CHIPS, 0, 0, tiled=True)
    mip, zmap = search(ids, spec, seen, across(seen))
    returned, mip, zmap = lax.optimization_barrier((returned, mip, zmap))
    refined = jnp.sum(returned, 0).reshape(16, 16)[:, :9]
    return (mip, zmap, refined)


def solution(mesh):
    inner = Mesh(mesh.devices.reshape(2, 4, 4, 2, 2), ("zl", "y", "x", "zh", "core"))
    every = ROWS_OF + COLS_OF
    placed = (
        P(ROWS_OF, COLS_OF),
        P(ROWS_OF, None, None),
        P(COLS_OF, None, None),
        P(every, None),
        P(every),
        P(every, None),
    )
    return jax.shard_map(
        body,
        mesh=inner,
        in_specs=placed,
        out_specs=(P(ROWS_OF, COLS_OF), P(ROWS_OF, COLS_OF), P(every, None)),
        check_vma=False,
    )
```

```python
import math

import jax
import jax.numpy as jnp
import numpy as np
from jax import lax
from jax.experimental import pallas as pl
from jax.experimental.pallas import tpu as pltpu
from jax.sharding import Mesh
from jax.sharding import PartitionSpec as P

L = 384
H = 192
Q = 96
SLABS = 64
ROWS = 40
WIDE = 1280
BF = jnp.bfloat16
F32 = jnp.float32
MB = 1024 * 1024
LIMIT = 62 * MB
ROWS_OF = ("zl", "y")
COLS_OF = ("x", "zh", "core")
CHIPS = ("zl", "y", "x", "zh")


def dot(a, b):
    return jnp.dot(a, b, preferred_element_type=F32)


def wave(a, b):
    angle = (np.multiply.outer(np.asarray(a), np.asarray(b)) % L) * (2.0 * math.pi / L)
    return np.cos(angle), np.sin(angle)


def bf(a):
    return np.asarray(a, np.float32).astype(jnp.bfloat16)


def make_tables():
    n = np.arange(L)
    cos, sin = wave(n, n)
    forward = np.concatenate([cos[:H], cos[H : H + 1], sin[1:H]], 0)
    halves = np.stack(
        [np.concatenate([forward[c * Q : c * Q + Q], forward[H + c * Q : H + c * Q + Q]], 0) for c in range(2)]
    )
    pair = np.concatenate([cos, sin], 1)
    inverse_cols = np.concatenate([pair, np.concatenate([-sin, cos], 1)], 0)
    weight = np.full((H,), 2.0)
    weight[0] = 1.0
    inverse_rows = np.concatenate([cos[:, :H] * weight, -2.0 * sin[:, :H]], 1)
    inverse_rows[:, H] = cos[:, H]
    reverse = np.zeros((L, L))
    reverse[(-n) % L, n] = 1.0
    pick = np.zeros((4, L, 128))
    for part in range(4):
        pick[part, n, 80 + 6 * part + n % 6] = 1.0
    lane = np.arange(128)
    field = np.zeros((128, 3, 128))
    for which, at in enumerate((0, 32, 64)):
        if which < 2:
            field[at : at + 16, which] = 128.0
            at += 16
        field[at : at + 16, which] = 1.0
    ac = lane % 16
    a, c = ac // 3 - 1, ac % 3 - 1
    comb = np.zeros((2, 3, L, 128))
    extra = np.zeros((SLABS, 2, 8, 128))
    for shift in (-1, 0, 1):
        kc, ks = wave(n, [shift])
        for part in range(4):
            at = 6 * part + 2 * (shift + 1)
            if part < 3:
                comb[0, part, :, at], comb[0, part, :, at + 1] = kc[:, 0], ks[:, 0]
                comb[1, part, :, at], comb[1, part, :, at + 1] = -ks[:, 0], kc[:, 0]
            else:
                kc, ks = kc[:, 0].reshape(SLABS, 6), ks[:, 0].reshape(SLABS, 6)
                extra[:, 0, :6, at], extra[:, 0, :6, at + 1] = kc, ks
                extra[:, 1, :6, at], extra[:, 1, :6, at + 1] = -ks, kc
    turn = np.zeros((SLABS, 16, L))
    widen = np.zeros((256, 16))
    last = np.zeros((SLABS, 2, 128, 128))
    for part in range(4):
        widen[6 * part : 6 * part + 6, part] = 1.0
        widen[128 + 6 * part : 128 + 6 * part + 6, 4 + part] = 1.0
    for s in range(SLABS):
        for part in range(4):
            k = s + 64 * part if part < 3 else H
            kc, ks = wave([k], n)
            turn[s, part], turn[s, 4 + part] = kc[0], ks[0]
            ca, sa = wave([k], a)
            w = 1.0 if k in (0, H) else 2.0
            for shift in (-1, 0, 1):
                at = 6 * part + 2 * (shift + 1)
                on = w * ((ac < 9) & (c == shift))
                last[s, 0, at], last[s, 0, at + 1] = on * ca[0], -on * sa[0]
                last[s, 1, at], last[s, 1, at + 1] = -on * sa[0], -on * ca[0]
    return dict(
        forward=bf(forward),
        halves=bf(halves),
        pair=bf(pair),
        inverse_cols=bf(inverse_cols),
        inverse_rows=bf(inverse_rows),
        reverse=bf(reverse),
        pick=bf(pick.reshape(4 * L, 128)),
        field=bf(field.reshape(128, 384)),
        comb=bf(comb.reshape(6 * L, 128)),
        extra=bf(extra.reshape(SLABS, 16, 128)),
        turn=bf(turn),
        widen=bf(widen),
        last=bf(last.reshape(SLABS, 256, 128)),
    )


TAB = make_tables()


def full_spec(shape):
    zeros = (0,) * len(shape)
    return pl.BlockSpec(shape, lambda i: zeros)


def place():
    blk = lax.axis_index("zl") * 4 + lax.axis_index("y")
    slab = blk * 8 + lax.axis_index("x") * 2 + lax.axis_index("zh")
    return blk, lax.axis_index("core"), slab


def iota(shape, dim):
    return lax.broadcasted_iota(jnp.int32, shape, dim)


def prepare_kernel(
    offsets,
    choice,
    owners,
    tile_hbm,
    bank_hbm,
    forward_hbm,
    pair_hbm,
    pick_hbm,
    msg,
    spec,
    flat,
    tile,
    ref,
    forward,
    pair,
    pick,
    sems,
):
    blk, core, _ = place()
    jobs = (
        (forward_hbm, forward),
        (tile_hbm, tile),
        (pair_hbm, pair),
        (bank_hbm.at[blk], ref),
        (pick_hbm, pick),
    )
    copies = [pltpu.make_async_copy(src, dst, sems.at[n]) for n, (src, dst) in enumerate(jobs)]
    for copy in copies:
        copy.start()

    r8 = iota((8, 16), 0)
    ox, oy = offsets[0:1], offsets[1:2]
    owner = owners[...]
    named = choice[...] * 8 + (owner >> 1) + 64 * ((owner & 1) ^ core)
    values = jnp.where(r8 == 4, named, 0)
    for n, value in enumerate((ox >> 7, ox & 127, oy >> 7, oy & 127)):
        values = jnp.where(r8 == n, value, values)
    wide = ((iota((16, 128), 1) & 15) == iota((16, 128), 0)).astype(BF)
    lined = dot(values.astype(F32).astype(BF), wide)
    lined = jnp.where((iota((8, 128), 1) >> 4) == iota((8, 128), 0), lined, 0.0)
    meta = jnp.sum(lined, axis=0, keepdims=True)

    rows64 = iota((SLABS, L), 0)
    owned = (iota((SLABS, L), 1) // 6) == rows64
    first_row = rows64 == 0
    for row in range(37, ROWS):
        flat[pl.ds(row, SLABS, stride=ROWS), :] = jnp.zeros((SLABS, 128), F32)
    copies[0].wait()
    lasts = []
    for which, image in enumerate((tile, ref)):
        copies[1 + 2 * which].wait()
        first = dot(forward[...], image[...]).astype(BF)
        if which == 0:
            copies[2].wait()
        second = dot(first, pair[...])
        real = second[:H, :L] - second[H:, L:]
        imag = -(second[:H, L:] + second[H:, :L])
        if which == 0:
            spec[0] = real.astype(BF)
            spec[1] = imag.astype(BF)
        for plane, (full, alone) in enumerate(((real, second[:64, :L]), (imag, -second[:64, L:]))):
            for part in range(3):
                block = full[64 * part : 64 * part + 64]
                if part == 0:
                    block = jnp.where(first_row, alone, block)
                for j in range(3):
                    row = 18 * which + 9 * plane + 3 * part + j
                    flat[pl.ds(row, SLABS, stride=ROWS), :] = block[:, 128 * j : 128 * j + 128]
        for last in (second[H : H + 1, :L], -second[H : H + 1, L:]):
            lasts.append(jnp.where(owned, jnp.broadcast_to(last, (SLABS, L)), 0.0).astype(BF))
    copies[4].wait()
    line = dot(jnp.concatenate(lasts, 1), pick[...])
    flat[pl.ds(36, SLABS, stride=ROWS), :] = line + meta
    msg[...] = flat[...].reshape(SLABS, ROWS, 128).astype(BF)


def prepare(offsets, choice, owners, tile, bank):
    held = pl.BlockSpec(memory_space=pltpu.HBM)
    return pl.pallas_call(
        prepare_kernel,
        out_shape=(
            jax.ShapeDtypeStruct((SLABS, ROWS, 128), BF),
            jax.ShapeDtypeStruct((2, H, L), BF),
        ),
        grid=(1,),
        in_specs=[full_spec((2, 16)), full_spec((1, 16)), full_spec((1, 16))] + [held] * 5,
        out_specs=[full_spec((SLABS, ROWS, 128)), full_spec((2, H, L))],
        scratch_shapes=[
            pltpu.VMEM((SLABS * ROWS, 128), F32),
            pltpu.VMEM((L, L), BF),
            pltpu.VMEM((L, L), BF),
            pltpu.VMEM((L, L), BF),
            pltpu.VMEM((L, 2 * L), BF),
            pltpu.VMEM((4 * L, 128), BF),
            pltpu.SemaphoreType.DMA((5,)),
        ],
        compiler_params=pltpu.CompilerParams(vmem_limit_bytes=LIMIT),
        cost_estimate=pl.CostEstimate(flops=1_000_000_000, bytes_accessed=4 * MB, transcendentals=0),
        name="prepare_spectra",
    )(offsets, choice, owners, tile, bank, TAB["forward"], TAB["pair"], TAB["pick"])


def template_kernel(template_hbm, halves_hbm, pair_hbm, half, template, rows_half, pair, sems):
    core = lax.axis_index("core")
    jobs = ((template_hbm.at[0], template), (halves_hbm.at[core], rows_half), (pair_hbm, pair))
    copies = [pltpu.make_async_copy(src, dst, sems.at[n]) for n, (src, dst) in enumerate(jobs)]
    for copy in copies:
        copy.start()
    copies[0].wait()
    values = template[...].astype(F32)
    count = 1.0 / (L * L)
    spread = values - jnp.sum(values) * count
    power = jnp.sum(spread * spread) * count
    scale = 1.0 / (L * jnp.sqrt(jnp.full((1, 1), power + 1e-06, F32)))
    normalized = (spread * scale).astype(BF)
    copies[1].wait()
    first = dot(rows_half[...], normalized).astype(BF)
    copies[2].wait()
    second = dot(first, pair[...])
    half[0] = (second[:Q, :L] - second[Q:, L:]).astype(BF)
    half[1] = (-(second[:Q, L:] + second[Q:, :L])).astype(BF)


def template_half(templates):
    held = pl.BlockSpec(memory_space=pltpu.HBM)
    return pl.pallas_call(
        template_kernel,
        out_shape=jax.ShapeDtypeStruct((2, Q, L), BF),
        grid=(1,),
        in_specs=[held] * 3,
        out_specs=full_spec((2, Q, L)),
        scratch_shapes=[
            pltpu.VMEM((L, L), BF),
            pltpu.VMEM((H, L), BF),
            pltpu.VMEM((L, 2 * L), BF),
            pltpu.SemaphoreType.DMA((3,)),
        ],
        compiler_params=pltpu.CompilerParams(vmem_limit_bytes=LIMIT),
        cost_estimate=pl.CostEstimate(flops=400_000_000, bytes_accessed=4 * MB, transcendentals=0),
        name="template_spectrum",
    )(templates, TAB["halves"], TAB["pair"])


MAIN = 6 * L
N_CAND = 1024


def refine_kernel(
    own_hbm, other_hbm, pair_hbm, field_hbm, comb_hbm, widen_hbm, turn_hbm, extra_hbm, last_hbm, out,
    own, other, pair, field, comb, widen, turn, extra, last,
    flat, tiles, refs, waves, ref_of, wave_of, both, turned, sems,
):
    slab = place()[2]
    jobs = (
        (other_hbm, other),
        (own_hbm, own),
        (pair_hbm, pair),
        (widen_hbm, widen),
        (turn_hbm.at[pl.ds(slab, 1)], turn),
        (extra_hbm.at[pl.ds(slab, 1)], extra),
        (field_hbm, field),
        (comb_hbm, comb),
        (last_hbm.at[pl.ds(slab, 1)], last),
    )
    copies = [pltpu.make_async_copy(src, dst, sems.at[n]) for n, (src, dst) in enumerate(jobs)]
    for copy in copies:
        copy.start()
    lane64 = iota((SLABS, 128), 1)

    def spread(base, target, rows):
        for col in range(18):
            target[rows, 128 * col : 128 * col + 128] = flat[pl.ds(base + col, SLABS, stride=ROWS), :].astype(
                target.dtype
            )
        line = flat[pl.ds(36, SLABS, stride=ROWS), :]
        for plane in range(2):
            at = 80 + (12 if base else 0) + 6 * plane
            moved = jnp.where(lane64 < 6, pltpu.roll(line, 128 - at, axis=1), 0.0)
            target[rows, MAIN + 128 * plane : MAIN + 128 * plane + 128] = moved.astype(target.dtype)
        return line

    copies[0].wait()
    flat[...] = other[...].astype(F32).reshape(SLABS * ROWS, 128)
    spread(18, refs, slice(64, 128))
    copies[1].wait()
    flat[...] = own[...].astype(F32).reshape(SLABS * ROWS, 128)
    spread(18, refs, slice(0, 64))
    meta = spread(0, tiles, slice(0, 64)).astype(BF)

    copies[2].wait()
    waves[:, : 2 * L] = pair[...]
    wanted = (iota((L, 128), 0) == iota((L, 128), 1) + 6 * slab).astype(BF)
    waves[:, 768:896] = dot(pair[:, :L], wanted).astype(BF)
    waves[:, 896:1024] = dot(pair[:, L:], wanted).astype(BF)
    copies[3].wait()
    copies[4].wait()
    copies[5].wait()
    turns = dot(widen[...], turn[0]).astype(BF)
    pad = jnp.zeros((112, 128), BF)
    ends = jnp.concatenate(
        [
            jnp.concatenate([extra[0, :8].astype(F32), jnp.zeros((8, 128), F32)], 0).astype(BF),
            pad,
            jnp.concatenate([extra[0, 8:].astype(F32), jnp.zeros((8, 128), F32)], 0).astype(BF),
            pad,
        ],
        0,
    )

    block = 256
    rowb = iota((block, 128), 0)
    laneb = iota((block, 128), 1)
    mine = (laneb & 15) == (rowb & 15)
    lanef = laneb.astype(F32)

    def gather(q):
        rows = pl.ds(block * q, block)
        repeat = iota((block, SLABS), 1) == 16 * q + (iota((block, SLABS), 0) >> 4)
        fields = dot(repeat.astype(BF), meta)
        spots = dot(jnp.where(mine, fields, 0.0).astype(BF), field[...])
        hot_x = jnp.concatenate([(lanef + 128.0 * j == spots[:, :128]).astype(BF) for j in range(3)], 1)
        hot_y = jnp.concatenate([(lanef + 128.0 * j == spots[:, 128:256]).astype(BF) for j in range(3)], 1)
        hot_t = (lanef == spots[:, 256:]).astype(BF)
        ref_of[rows, :] = dot(hot_t, refs[...]).astype(BF)
        wave_of[rows, :] = dot(hot_y, waves[...]).astype(BF)
        turned[rows, :] = lax.dot_general(
            hot_x, turns, (((1,), (1,)), ((), ())), preferred_element_type=F32
        ).astype(BF)

    def multiply(q):
        eight = pl.ds(8 * q, 8)
        for size, wave_at, places in (
            (L, 0, tuple((L * part, 3 * L + L * part) for part in range(3))),
            (128, 2 * L, ((MAIN, MAIN + 128),)),
        ):
            for at_r, at_i in places:
                tiles_r = tiles[eight, at_r : at_r + size]
                tiles_i = tiles[eight, at_i : at_i + size]
                for j in range(8):
                    rows = pl.ds(128 * q + 16 * j, 16)
                    cos_y = wave_of[rows, wave_at : wave_at + size].astype(F32)
                    sin_y = wave_of[rows, wave_at + size : wave_at + 2 * size].astype(F32)
                    tile_r, tile_i = tiles_r[j : j + 1], tiles_i[j : j + 1]
                    ref_r = ref_of[rows, at_r : at_r + size].astype(F32)
                    ref_i = ref_of[rows, at_i : at_i + size].astype(F32)
                    prod_r = tile_r * ref_r + tile_i * ref_i
                    prod_i = tile_i * ref_r - tile_r * ref_i
                    both[rows, at_r : at_r + size] = (prod_r * cos_y - prod_i * sin_y).astype(BF)
                    both[rows, at_i : at_i + size] = (prod_r * sin_y + prod_i * cos_y).astype(BF)

    kept = (laneb >> 4) == (rowb & 7)

    def finish(q):
        rows = pl.ds(block * q, block)
        sums = dot(both[rows, :MAIN], comb[...]) + dot(both[rows, MAIN:], ends)
        kappa = turned[rows, :].astype(F32)
        mixed = jnp.concatenate([(sums * kappa[:, :128]).astype(BF), (sums * kappa[:, 128:]).astype(BF)], 1)
        total = jnp.where(kept, dot(mixed, last[0]) * (1.0 / (L * L)), 0.0)
        to = pl.ds(block // 8 * q, block // 8)
        out[to, :] = jnp.sum(total.reshape(block // 8, 8, 128), axis=1)

    count = N_CAND // block
    for n in (6, 7, 8):
        copies[n].wait()
    gather(0)
    for q in range(count):
        if q + 1 < count:
            gather(q + 1)
        for p in range(block // 128):
            multiply(block // 128 * q + p)
        finish(q)


def refine(own, other):
    held = pl.BlockSpec(memory_space=pltpu.HBM)
    return pl.pallas_call(
        refine_kernel,
        out_shape=jax.ShapeDtypeStruct((128, 128), F32),
        grid=(1,),
        in_specs=[held] * 9,
        out_specs=full_spec((128, 128)),
        scratch_shapes=[
            pltpu.VMEM((SLABS, ROWS, 128), BF),
            pltpu.VMEM((SLABS, ROWS, 128), BF),
            pltpu.VMEM((L, 2 * L), BF),
            pltpu.VMEM((128, 384), BF),
            pltpu.VMEM((MAIN, 128), BF),
            pltpu.VMEM((256, 16), BF),
            pltpu.VMEM((1, 16, L), BF),
            pltpu.VMEM((1, 16, 128), BF),
            pltpu.VMEM((1, 256, 128), BF),
            pltpu.VMEM((SLABS * ROWS, 128), F32),
            pltpu.VMEM((SLABS, MAIN + 256), F32),
            pltpu.VMEM((128, MAIN + 256), BF),
            pltpu.VMEM((L, 1024), BF),
            pltpu.VMEM((N_CAND, MAIN + 256), BF),
            pltpu.VMEM((N_CAND, 1024), BF),
            pltpu.VMEM((N_CAND, MAIN + 256), BF),
            pltpu.VMEM((N_CAND, 256), BF),
            pltpu.SemaphoreType.DMA((9,)),
        ],
        compiler_params=pltpu.CompilerParams(vmem_limit_bytes=LIMIT),
        cost_estimate=pl.CostEstimate(flops=9_000_000_000, bytes_accessed=4 * MB, transcendentals=0),
        name="refine_slab",
    )(own, other, TAB["pair"], TAB["field"], TAB["comb"], TAB["widen"], TAB["turn"], TAB["extra"], TAB["last"])


def search_kernel(
    spec_hbm, o0, o1, o2, o3, p0, p1, p2, p3, cols_hbm, rows_hbm, reverse_hbm, mip, zmap,
    spec, own, oth, own_top, oth_top, cols, rows, reverse, prod, total, square, sems,
):
    core = lax.axis_index("core")
    owns, others = (o0, o1, o2, o3), (p0, p1, p2, p3)
    jobs = [(spec_hbm, spec), (reverse_hbm, reverse)]
    for p in range(4):
        jobs.append((owns[p].at[:, :, pl.ds(0, 16), :], own_top.at[pl.ds(2 * p, 2)]))
        jobs.append((others[p].at[:, :, pl.ds(0, 16), :], oth_top.at[pl.ds(2 * p, 2)]))
    tops = len(jobs)
    for p in range(4):
        jobs.append((owns[p], own.at[pl.ds(2 * p, 2)]))
        jobs.append((others[p], oth.at[pl.ds(2 * p, 2)]))
        if p == 0:
            jobs += [(cols_hbm, cols), (rows_hbm, rows)]
    copies = [pltpu.make_async_copy(src, dst, sems.at[n]) for n, (src, dst) in enumerate(jobs)]
    for copy in copies:
        copy.start()

    row16 = iota((16, L), 0)
    zero = jnp.zeros((16, L), F32)
    ends_r, ends_i = zero, zero
    for n in range(tops):
        copies[n].wait()
    for n in range(8):
        top_r = jnp.where(core == 0, own_top[n, 0].astype(F32), oth_top[n, 0].astype(F32))
        top_i = jnp.where(core == 0, own_top[n, 1].astype(F32), oth_top[n, 1].astype(F32))
        ends_r = jnp.where(row16 == n, top_r[0:1], ends_r)
        ends_i = jnp.where(row16 == n, top_i[0:1], ends_i)
    ends_r = jnp.where(row16 == 8, spec[0, :16].astype(F32)[0:1], ends_r)
    ends_i = jnp.where(row16 == 8, spec[1, :16].astype(F32)[0:1], ends_i)
    back = dot(jnp.concatenate([ends_r, ends_i], 0).astype(BF), reverse[...])
    back_r, back_i = back[:16], back[16:]
    low_r, low_i = 0.5 * (ends_r + back_r), 0.5 * (ends_i - back_i)
    top_r, top_i = -0.5 * (ends_i + back_i), 0.5 * (ends_r - back_r)

    def cross(a_r, a_i):
        s_r, s_i = a_r[8:9], a_i[8:9]
        return s_r * a_r + s_i * a_i, s_i * a_r - s_r * a_i

    low = cross(low_r, low_i)
    top = cross(top_r, top_i)
    line_r = low[0] - top[1]
    line_i = low[1] + top[0]

    def products(p):
        for n in (2 * p, 2 * p + 1):
            for ref, half in ((own, core), (oth, 1 - core)):
                for r in range(0, Q, 16):
                    where = pl.ds(pl.multiple_of(half * Q + r, 16), 16)
                    tile_r, tile_i = spec[0, where, :].astype(F32), spec[1, where, :].astype(F32)
                    t_r, t_i = ref[n, 0, r : r + 16].astype(F32), ref[n, 1, r : r + 16].astype(F32)
                    p_r = tile_r * t_r + tile_i * t_i
                    p_i = tile_i * t_r - tile_r * t_i
                    if r == 0:
                        lead = (row16 + half) == 0
                        p_r = jnp.where(lead, line_r[n : n + 1], p_r)
                        p_i = jnp.where(lead, line_i[n : n + 1], p_i)
                    prod[n, where, :L] = p_r.astype(BF)
                    prod[n, where, L:] = p_i.astype(BF)

    copies[tops].wait()
    copies[tops + 1].wait()
    products(0)
    copies[tops + 2].wait()
    copies[tops + 3].wait()
    for p in range(4):
        if p < 3:
            copies[tops + 4 + 2 * p].wait()
            copies[tops + 5 + 2 * p].wait()
            products(p + 1)
        middle = dot(prod[2 * p : 2 * p + 2].reshape(2 * H, 2 * L), cols[...]).astype(BF)
        both = []
        for k in range(2):
            part = middle[H * k : H * k + H]
            both.append(jnp.concatenate([part[:, :L], part[:, L:]], 0))
        corr = dot(rows[...], jnp.concatenate(both, 1)) * (1.0 / (L * L))
        one, two = corr[:, :L], corr[:, L:]
        largest = jnp.maximum(one, two)
        summed = one + two
        powers = one * one + two * two
        if p == 0:
            mip[...] = largest
            total[...] = summed
            square[...] = powers
        elif p < 3:
            mip[...] = jnp.maximum(mip[...], largest)
            total[...] += summed
            square[...] += powers
        else:
            largest = jnp.maximum(mip[...], largest)
            mean = (total[...] + summed) * 0.125
            var = (square[...] + powers) * 0.125 - mean * mean
            mip[...] = largest
            zmap[...] = (largest - mean) * lax.rsqrt(jnp.maximum(var, 0.25))


def search(spec, owns, others):
    held = pl.BlockSpec(memory_space=pltpu.HBM)
    return pl.pallas_call(
        search_kernel,
        out_shape=(jax.ShapeDtypeStruct((L, L), F32), jax.ShapeDtypeStruct((L, L), F32)),
        grid=(1,),
        in_specs=[held] * 12,
        out_specs=[full_spec((L, L)), full_spec((L, L))],
        scratch_shapes=[
            pltpu.VMEM((2, H, L), BF),
            pltpu.VMEM((8, 2, Q, L), BF),
            pltpu.VMEM((8, 2, Q, L), BF),
            pltpu.VMEM((8, 2, 16, L), BF),
            pltpu.VMEM((8, 2, 16, L), BF),
            pltpu.VMEM((2 * L, 2 * L), BF),
            pltpu.VMEM((L, L), BF),
            pltpu.VMEM((L, L), BF),
            pltpu.VMEM((8, H, 2 * L), BF),
            pltpu.VMEM((L, L), F32),
            pltpu.VMEM((L, L), F32),
            pltpu.SemaphoreType.DMA((20,)),
        ],
        compiler_params=pltpu.CompilerParams(vmem_limit_bytes=LIMIT),
        cost_estimate=pl.CostEstimate(flops=4_000_000_000, bytes_accessed=6 * MB, transcendentals=0),
        name="search_templates",
    )(spec, *owns, *others, TAB["inverse_cols"], TAB["inverse_rows"], TAB["reverse"])


def ring(count, step):
    return [(i, (i + step) % count) for i in range(count)]


def body(micrograph, templates, ref_bank, peak_offsets, peak_template, owners):
    def across(array):
        return lax.ppermute(array, "core", ring(2, 1))

    message, spec = prepare(
        peak_offsets.T, peak_template.reshape(1, 16), owners.reshape(1, 16), micrograph, ref_bank
    )
    arrived = lax.all_to_all(message, CHIPS, 0, 0, tiled=True)
    half = template_half(templates)
    near = lax.ppermute(half, "zl", ring(2, 1))
    arrived, half, near = lax.optimization_barrier((arrived, half, near))
    both = jnp.stack([half, near])
    owns = [both] + [lax.ppermute(both, "y", ring(4, step)) for step in (1, 3, 2)]
    scores = refine(arrived, across(arrived))
    after, owns = lax.optimization_barrier((scores, owns))
    returned = lax.all_to_all(scores.reshape(SLABS, 2, 128), CHIPS, 0, 0, tiled=True)
    mip, zmap = search(spec, owns, [across(one) for one in owns])
    returned, mip, zmap, after = lax.optimization_barrier((returned, mip, zmap, after))
    refined = jnp.sum(returned, 0).reshape(16, 16)[:, :9]
    return (mip, zmap, refined)


def solution(mesh):
    inner = Mesh(mesh.devices.reshape(2, 4, 4, 2, 2), ("zl", "y", "x", "zh", "core"))
    every = ROWS_OF + COLS_OF
    placed = (
        P(ROWS_OF, COLS_OF),
        P(ROWS_OF, None, None),
        P(COLS_OF, None, None),
        P(every, None),
        P(every),
        P(every, None),
    )
    return jax.shard_map(
        body,
        mesh=inner,
        in_specs=placed,
        out_specs=(P(ROWS_OF, COLS_OF), P(ROWS_OF, COLS_OF), P(every, None)),
        check_vma=False,
    )
```

```python
import math

import jax
import jax.numpy as jnp
import numpy as np
from jax import lax
from jax.experimental import pallas as pl
from jax.experimental.pallas import tpu as pltpu
from jax.sharding import Mesh
from jax.sharding import PartitionSpec as P

L = 384
H = 192
Q = 96
SLABS = 64
ROWS = 40
WIDE = 1280
BF = jnp.bfloat16
F32 = jnp.float32
MB = 1024 * 1024
LIMIT = 62 * MB
ROWS_OF = ("zl", "y")
COLS_OF = ("x", "zh", "core")
CHIPS = ("zl", "y", "x", "zh")


def dot(a, b):
    return jnp.dot(a, b, preferred_element_type=F32)


def wave(a, b):
    angle = (np.multiply.outer(np.asarray(a), np.asarray(b)) % L) * (2.0 * math.pi / L)
    return np.cos(angle), np.sin(angle)


def bf(a):
    return np.asarray(a, np.float32).astype(jnp.bfloat16)


def make_tables():
    n = np.arange(L)
    cos, sin = wave(n, n)
    order = np.concatenate([np.arange(0, H, 2), np.arange(1, H, 2)])
    forward = np.concatenate([cos[order], cos[H : H + 1], sin[order[1:]]], 0)
    halves = np.stack(
        [np.concatenate([forward[c * Q : c * Q + Q], forward[H + c * Q : H + c * Q + Q]], 0) for c in range(2)]
    )
    pair = np.concatenate([cos, sin], 1)
    inverse_cols = np.concatenate([pair, np.concatenate([-sin, cos], 1)], 0)
    weight = np.full((H,), 2.0)
    weight[0] = 1.0
    back_cos, back_sin = cos[:H, order] * weight, -2.0 * sin[:H, order]
    back_sin[:, 0] = cos[:H, H]
    inverse_rows = np.stack(
        [np.concatenate([back_cos[:, Q * c : Q * c + Q], back_sin[:, Q * c : Q * c + Q]], 1) for c in range(2)]
    )
    reverse = np.zeros((L, L))
    reverse[(-n) % L, n] = 1.0
    pick = np.zeros((4, L, 128))
    for part in range(4):
        pick[part, n, 80 + 6 * part + n % 6] = 1.0
    lane = np.arange(128)
    field = np.zeros((128, 3, 128))
    for which, at in enumerate((0, 32, 64)):
        if which < 2:
            field[at : at + 16, which] = 128.0
            at += 16
        field[at : at + 16, which] = 1.0
    ac = lane % 16
    a, c = ac // 3 - 1, ac % 3 - 1
    comb = np.zeros((2, 3, L, 128))
    extra = np.zeros((SLABS, 2, 8, 128))
    for shift in (-1, 0, 1):
        kc, ks = wave(n, [shift])
        for part in range(4):
            at = 6 * part + 2 * (shift + 1)
            if part < 3:
                comb[0, part, :, at], comb[0, part, :, at + 1] = kc[:, 0], ks[:, 0]
                comb[1, part, :, at], comb[1, part, :, at + 1] = -ks[:, 0], kc[:, 0]
            else:
                kc, ks = kc[:, 0].reshape(SLABS, 6), ks[:, 0].reshape(SLABS, 6)
                extra[:, 0, :6, at], extra[:, 0, :6, at + 1] = kc, ks
                extra[:, 1, :6, at], extra[:, 1, :6, at + 1] = -ks, kc
    turn = np.zeros((SLABS, 16, L))
    widen = np.zeros((256, 16))
    last = np.zeros((SLABS, 2, 128, 128))
    for part in range(4):
        widen[6 * part : 6 * part + 6, part] = 1.0
        widen[128 + 6 * part : 128 + 6 * part + 6, 4 + part] = 1.0
    for s in range(SLABS):
        for part in range(4):
            k = order[s + 64 * part] if part < 3 else H
            kc, ks = wave([k], n)
            turn[s, part], turn[s, 4 + part] = kc[0], ks[0]
            ca, sa = wave([k], a)
            w = 1.0 if k in (0, H) else 2.0
            for shift in (-1, 0, 1):
                at = 6 * part + 2 * (shift + 1)
                on = w * ((ac < 9) & (c == shift))
                last[s, 0, at], last[s, 0, at + 1] = on * ca[0], -on * sa[0]
                last[s, 1, at], last[s, 1, at + 1] = -on * sa[0], -on * ca[0]
    return dict(
        forward=bf(forward),
        halves=bf(halves),
        pair=bf(pair),
        inverse_cols=bf(inverse_cols),
        inverse_rows=bf(inverse_rows),
        reverse=bf(reverse),
        pick=bf(pick.reshape(4 * L, 128)),
        field=bf(field.reshape(128, 384)),
        comb=bf(comb.reshape(6 * L, 128)),
        extra=bf(extra.reshape(SLABS, 16, 128)),
        turn=bf(turn),
        widen=bf(widen),
        last=bf(last.reshape(SLABS, 256, 128)),
    )


TAB = make_tables()


def full_spec(shape):
    zeros = (0,) * len(shape)
    return pl.BlockSpec(shape, lambda i: zeros)


def place():
    blk = lax.axis_index("zl") * 4 + lax.axis_index("y")
    slab = blk * 8 + lax.axis_index("x") * 2 + lax.axis_index("zh")
    return blk, lax.axis_index("core"), slab


def iota(shape, dim):
    return lax.broadcasted_iota(jnp.int32, shape, dim)


def prepare_kernel(
    offsets,
    choice,
    owners,
    tile_hbm,
    bank_hbm,
    forward_hbm,
    pair_hbm,
    pick_hbm,
    msg,
    spec,
    flat,
    tile,
    ref,
    forward,
    pair,
    pick,
    sems,
):
    blk, core, _ = place()
    jobs = (
        (forward_hbm, forward),
        (tile_hbm, tile),
        (pair_hbm, pair),
        (bank_hbm.at[blk], ref),
        (pick_hbm, pick),
    )
    copies = [pltpu.make_async_copy(src, dst, sems.at[n]) for n, (src, dst) in enumerate(jobs)]
    for copy in copies:
        copy.start()

    r8 = iota((8, 16), 0)
    ox, oy = offsets[0:1], offsets[1:2]
    owner = owners[...]
    named = choice[...] * 8 + (owner >> 1) + 64 * ((owner & 1) ^ core)
    values = jnp.where(r8 == 4, named, 0)
    for n, value in enumerate((ox >> 7, ox & 127, oy >> 7, oy & 127)):
        values = jnp.where(r8 == n, value, values)
    wide = ((iota((16, 128), 1) & 15) == iota((16, 128), 0)).astype(BF)
    lined = dot(values.astype(F32).astype(BF), wide)
    lined = jnp.where((iota((8, 128), 1) >> 4) == iota((8, 128), 0), lined, 0.0)
    meta = jnp.sum(lined, axis=0, keepdims=True)

    rows64 = iota((SLABS, L), 0)
    owned = (iota((SLABS, L), 1) // 6) == rows64
    first_row = rows64 == 0
    for row in range(37, ROWS):
        flat[pl.ds(row, SLABS, stride=ROWS), :] = jnp.zeros((SLABS, 128), F32)
    copies[0].wait()
    lasts = []
    for which, image in enumerate((tile, ref)):
        copies[1 + 2 * which].wait()
        first = dot(forward[...], image[...]).astype(BF)
        if which == 0:
            copies[2].wait()
        second = dot(first, pair[...])
        real = second[:H, :L] - second[H:, L:]
        imag = -(second[:H, L:] + second[H:, :L])
        if which == 0:
            spec[0] = real.astype(BF)
            spec[1] = imag.astype(BF)
        for plane, (full, alone) in enumerate(((real, second[:64, :L]), (imag, -second[:64, L:]))):
            for part in range(3):
                block = full[64 * part : 64 * part + 64]
                if part == 0:
                    block = jnp.where(first_row, alone, block)
                for j in range(3):
                    row = 18 * which + 9 * plane + 3 * part + j
                    flat[pl.ds(row, SLABS, stride=ROWS), :] = block[:, 128 * j : 128 * j + 128]
        for last in (second[H : H + 1, :L], -second[H : H + 1, L:]):
            lasts.append(jnp.where(owned, jnp.broadcast_to(last, (SLABS, L)), 0.0).astype(BF))
    copies[4].wait()
    line = dot(jnp.concatenate(lasts, 1), pick[...])
    flat[pl.ds(36, SLABS, stride=ROWS), :] = line + meta
    msg[...] = flat[...].reshape(SLABS, ROWS, 128).astype(BF)


def prepare(offsets, choice, owners, tile, bank):
    held = pl.BlockSpec(memory_space=pltpu.HBM)
    return pl.pallas_call(
        prepare_kernel,
        out_shape=(
            jax.ShapeDtypeStruct((SLABS, ROWS, 128), BF),
            jax.ShapeDtypeStruct((2, H, L), BF),
        ),
        grid=(1,),
        in_specs=[full_spec((2, 16)), full_spec((1, 16)), full_spec((1, 16))] + [held] * 5,
        out_specs=[full_spec((SLABS, ROWS, 128)), full_spec((2, H, L))],
        scratch_shapes=[
            pltpu.VMEM((SLABS * ROWS, 128), F32),
            pltpu.VMEM((L, L), BF),
            pltpu.VMEM((L, L), BF),
            pltpu.VMEM((L, L), BF),
            pltpu.VMEM((L, 2 * L), BF),
            pltpu.VMEM((4 * L, 128), BF),
            pltpu.SemaphoreType.DMA((5,)),
        ],
        compiler_params=pltpu.CompilerParams(vmem_limit_bytes=62 * MB),
        cost_estimate=pl.CostEstimate(flops=1_000_000_000, bytes_accessed=4 * MB, transcendentals=0),
        name="prepare_spectra",
    )(offsets, choice, owners, tile, bank, TAB["forward"], TAB["pair"], TAB["pick"])


def template_kernel(template_hbm, halves_hbm, pair_hbm, half, template, rows_half, pair, sems):
    core = lax.axis_index("core")
    jobs = ((template_hbm.at[0], template), (halves_hbm.at[core], rows_half), (pair_hbm, pair))
    copies = [pltpu.make_async_copy(src, dst, sems.at[n]) for n, (src, dst) in enumerate(jobs)]
    for copy in copies:
        copy.start()
    copies[0].wait()
    values = template[...].astype(F32)
    count = 1.0 / (L * L)
    spread = values - jnp.sum(values) * count
    power = jnp.sum(spread * spread) * count
    scale = 1.0 / (L * jnp.sqrt(jnp.full((1, 1), power + 1e-06, F32)))
    normalized = (spread * scale).astype(BF)
    copies[1].wait()
    first = dot(rows_half[...], normalized).astype(BF)
    copies[2].wait()
    second = dot(first, pair[...])
    half[0] = (second[:Q, :L] - second[Q:, L:]).astype(BF)
    half[1] = (-(second[:Q, L:] + second[Q:, :L])).astype(BF)


def template_half(templates):
    held = pl.BlockSpec(memory_space=pltpu.HBM)
    return pl.pallas_call(
        template_kernel,
        out_shape=jax.ShapeDtypeStruct((2, Q, L), BF),
        grid=(1,),
        in_specs=[held] * 3,
        out_specs=full_spec((2, Q, L)),
        scratch_shapes=[
            pltpu.VMEM((L, L), BF),
            pltpu.VMEM((H, L), BF),
            pltpu.VMEM((L, 2 * L), BF),
            pltpu.SemaphoreType.DMA((3,)),
        ],
        compiler_params=pltpu.CompilerParams(vmem_limit_bytes=36 * MB),
        cost_estimate=pl.CostEstimate(flops=400_000_000, bytes_accessed=4 * MB, transcendentals=0),
        name="template_spectrum",
    )(templates, TAB["halves"], TAB["pair"])


MAIN = 6 * L
N_CAND = 1024


def refine_kernel(
    own_hbm, other_hbm, pair_hbm, field_hbm, comb_hbm, widen_hbm, turn_hbm, extra_hbm, last_hbm, out,
    own, other, pair, field, comb, widen, turn, extra, last,
    flat, tiles, refs, waves, ref_of, wave_of, both, turned, sems,
):
    slab = place()[2]
    jobs = (
        (pair_hbm, pair),
        (widen_hbm, widen),
        (turn_hbm.at[pl.ds(slab, 1)], turn),
        (extra_hbm.at[pl.ds(slab, 1)], extra),
        (other_hbm, other),
        (own_hbm, own),
        (field_hbm, field),
        (comb_hbm, comb),
        (last_hbm.at[pl.ds(slab, 1)], last),
    )
    copies = [pltpu.make_async_copy(src, dst, sems.at[n]) for n, (src, dst) in enumerate(jobs)]
    for copy in copies:
        copy.start()
    lane64 = iota((SLABS, 128), 1)

    def spread(base, target, rows):
        for col in range(18):
            target[rows, 128 * col : 128 * col + 128] = flat[pl.ds(base + col, SLABS, stride=ROWS), :].astype(
                target.dtype
            )
        line = flat[pl.ds(36, SLABS, stride=ROWS), :]
        for plane in range(2):
            at = 80 + (12 if base else 0) + 6 * plane
            moved = jnp.where(lane64 < 6, pltpu.roll(line, 128 - at, axis=1), 0.0)
            target[rows, MAIN + 128 * plane : MAIN + 128 * plane + 128] = moved.astype(target.dtype)
        return line

    copies[0].wait()
    waves[:, : 2 * L] = pair[...]
    wanted = (iota((L, 128), 0) == iota((L, 128), 1) + 6 * slab).astype(BF)
    waves[:, 768:896] = dot(pair[:, :L], wanted).astype(BF)
    waves[:, 896:1024] = dot(pair[:, L:], wanted).astype(BF)
    copies[1].wait()
    copies[2].wait()
    copies[3].wait()
    turns = dot(widen[...], turn[0]).astype(BF)
    pad = jnp.zeros((112, 128), BF)
    ends = jnp.concatenate(
        [
            jnp.concatenate([extra[0, :8].astype(F32), jnp.zeros((8, 128), F32)], 0).astype(BF),
            pad,
            jnp.concatenate([extra[0, 8:].astype(F32), jnp.zeros((8, 128), F32)], 0).astype(BF),
            pad,
        ],
        0,
    )

    copies[4].wait()
    flat[...] = other[...].astype(F32).reshape(SLABS * ROWS, 128)
    spread(18, refs, slice(64, 128))
    copies[5].wait()
    flat[...] = own[...].astype(F32).reshape(SLABS * ROWS, 128)
    spread(18, refs, slice(0, 64))
    meta = spread(0, tiles, slice(0, 64)).astype(BF)

    block = 256
    rowb = iota((block, 128), 0)
    laneb = iota((block, 128), 1)
    mine = (laneb & 15) == (rowb & 15)
    lanef = laneb.astype(F32)

    def gather(q):
        rows = pl.ds(block * q, block)
        repeat = iota((block, SLABS), 1) == 16 * q + (iota((block, SLABS), 0) >> 4)
        fields = dot(repeat.astype(BF), meta)
        spots = dot(jnp.where(mine, fields, 0.0).astype(BF), field[...])
        hot_x = jnp.concatenate([(lanef + 128.0 * j == spots[:, :128]).astype(BF) for j in range(3)], 1)
        hot_y = jnp.concatenate([(lanef + 128.0 * j == spots[:, 128:256]).astype(BF) for j in range(3)], 1)
        hot_t = (lanef == spots[:, 256:]).astype(BF)
        ref_of[rows, :] = dot(hot_t, refs[...])
        wave_of[rows, :] = dot(hot_y, waves[...])
        turned[rows, :] = lax.dot_general(
            hot_x, turns, (((1,), (1,)), ((), ())), preferred_element_type=F32
        ).astype(BF)

    def multiply(q):
        for size, wave_at, places in (
            (L, 0, tuple((L * part, 3 * L + L * part) for part in range(3))),
            (128, 2 * L, ((MAIN, MAIN + 128),)),
        ):
            for j in range(8):
                rows = pl.ds(128 * q + 16 * j, 16)
                for m in range(0, size, 128):
                    cos_y = wave_of[rows, wave_at + m : wave_at + m + 128].astype(F32)
                    sin_y = wave_of[rows, wave_at + size + m : wave_at + size + m + 128].astype(F32)
                    for at_r, at_i in places:
                        lanes_r, lanes_i = slice(at_r + m, at_r + m + 128), slice(at_i + m, at_i + m + 128)
                        tile_r = tiles[8 * q + j : 8 * q + j + 1, lanes_r]
                        tile_i = tiles[8 * q + j : 8 * q + j + 1, lanes_i]
                        ref_r = ref_of[rows, lanes_r].astype(F32)
                        ref_i = ref_of[rows, lanes_i].astype(F32)
                        prod_r = tile_r * ref_r + tile_i * ref_i
                        prod_i = tile_i * ref_r - tile_r * ref_i
                        both[rows, lanes_r] = (prod_r * cos_y - prod_i * sin_y).astype(BF)
                        both[rows, lanes_i] = (prod_r * sin_y + prod_i * cos_y).astype(BF)

    kept = (laneb >> 4) == (rowb & 7)

    def finish(q):
        rows = pl.ds(block * q, block)
        sums = dot(both[rows, :MAIN], comb[...]) + dot(both[rows, MAIN:], ends)
        kappa = turned[rows, :].astype(F32)
        mixed = jnp.concatenate([(sums * kappa[:, :128]).astype(BF), (sums * kappa[:, 128:]).astype(BF)], 1)
        total = jnp.where(kept, dot(mixed, last[0]) * (1.0 / (L * L)), 0.0)
        to = pl.ds(block // 8 * q, block // 8)
        out[to, :] = jnp.sum(total.reshape(block // 8, 8, 128), axis=1)

    count = N_CAND // block
    for n in (6, 7, 8):
        copies[n].wait()
    gather(0)
    for q in range(count):
        if q + 1 < count:
            gather(q + 1)
        for p in range(block // 128):
            multiply(block // 128 * q + p)
        finish(q)


def refine(own, other):
    held = pl.BlockSpec(memory_space=pltpu.HBM)
    return pl.pallas_call(
        refine_kernel,
        out_shape=jax.ShapeDtypeStruct((128, 128), F32),
        grid=(1,),
        in_specs=[pl.BlockSpec(memory_space=pl.ANY)] * 2 + [held] * 7,
        out_specs=full_spec((128, 128)),
        scratch_shapes=[
            pltpu.VMEM((SLABS, ROWS, 128), BF),
            pltpu.VMEM((SLABS, ROWS, 128), BF),
            pltpu.VMEM((L, 2 * L), BF),
            pltpu.VMEM((128, 384), BF),
            pltpu.VMEM((MAIN, 128), BF),
            pltpu.VMEM((256, 16), BF),
            pltpu.VMEM((1, 16, L), BF),
            pltpu.VMEM((1, 16, 128), BF),
            pltpu.VMEM((1, 256, 128), BF),
            pltpu.VMEM((SLABS * ROWS, 128), F32),
            pltpu.VMEM((SLABS, MAIN + 256), F32),
            pltpu.VMEM((128, MAIN + 256), BF),
            pltpu.VMEM((L, 1024), BF),
            pltpu.VMEM((N_CAND, MAIN + 256), F32),
            pltpu.VMEM((N_CAND, 1024), F32),
            pltpu.VMEM((N_CAND, MAIN + 256), BF),
            pltpu.VMEM((N_CAND, 256), BF),
            pltpu.SemaphoreType.DMA((9,)),
        ],
        compiler_params=pltpu.CompilerParams(vmem_limit_bytes=62 * MB),
        cost_estimate=pl.CostEstimate(flops=9_000_000_000, bytes_accessed=4 * MB, transcendentals=0),
        name="refine_slab",
    )(own, other, TAB["pair"], TAB["field"], TAB["comb"], TAB["widen"], TAB["turn"], TAB["extra"], TAB["last"])


def search_kernel(
    spec_hbm, o0, o1, o2, o3, p0, p1, p2, p3, cols_hbm, rows_hbm, reverse_hbm, mip, zmap,
    spec, own, oth, own_top, oth_top, cols, rows, reverse, prod, total, square, sems,
):
    core = lax.axis_index("core")
    owns, others = (o0, o1, o2, o3), (p0, p1, p2, p3)
    jobs = [(spec_hbm, spec), (reverse_hbm, reverse)]
    for p in range(4):
        jobs.append((owns[p].at[:, :, pl.ds(0, 16), :], own_top.at[pl.ds(2 * p, 2)]))
        jobs.append((others[p].at[:, :, pl.ds(0, 16), :], oth_top.at[pl.ds(2 * p, 2)]))
    tops = len(jobs)
    for p in range(4):
        jobs.append((owns[p], own.at[pl.ds(2 * p, 2)]))
        jobs.append((others[p], oth.at[pl.ds(2 * p, 2)]))
        if p == 0:
            jobs += [(cols_hbm, cols), (rows_hbm, rows)]
    copies = [pltpu.make_async_copy(src, dst, sems.at[n]) for n, (src, dst) in enumerate(jobs)]
    for copy in copies:
        copy.start()

    row16 = iota((16, L), 0)
    zero = jnp.zeros((16, L), F32)
    ends_r, ends_i = zero, zero
    for n in range(tops):
        copies[n].wait()
    for n in range(8):
        top_r = jnp.where(core == 0, own_top[n, 0].astype(F32), oth_top[n, 0].astype(F32))
        top_i = jnp.where(core == 0, own_top[n, 1].astype(F32), oth_top[n, 1].astype(F32))
        ends_r = jnp.where(row16 == n, top_r[0:1], ends_r)
        ends_i = jnp.where(row16 == n, top_i[0:1], ends_i)
    ends_r = jnp.where(row16 == 8, spec[0, :16].astype(F32)[0:1], ends_r)
    ends_i = jnp.where(row16 == 8, spec[1, :16].astype(F32)[0:1], ends_i)
    back = dot(jnp.concatenate([ends_r, ends_i], 0).astype(BF), reverse[...])
    back_r, back_i = back[:16], back[16:]
    low_r, low_i = 0.5 * (ends_r + back_r), 0.5 * (ends_i - back_i)
    top_r, top_i = -0.5 * (ends_i + back_i), 0.5 * (ends_r - back_r)

    def cross(a_r, a_i):
        s_r, s_i = a_r[8:9], a_i[8:9]
        return s_r * a_r + s_i * a_i, s_i * a_r - s_r * a_i

    low = cross(low_r, low_i)
    top = cross(top_r, top_i)
    line_r = low[0] - top[1]
    line_i = low[1] + top[0]

    def products(p):
        for n in (2 * p, 2 * p + 1):
            for ref, half in ((own, core), (oth, 1 - core)):
                for r in range(0, Q, 16):
                    where = pl.ds(pl.multiple_of(half * Q + r, 16), 16)
                    tile_r, tile_i = spec[0, where, :].astype(F32), spec[1, where, :].astype(F32)
                    t_r, t_i = ref[n, 0, r : r + 16].astype(F32), ref[n, 1, r : r + 16].astype(F32)
                    p_r = tile_r * t_r + tile_i * t_i
                    p_i = tile_i * t_r - tile_r * t_i
                    if r == 0:
                        lead = (row16 + half) == 0
                        p_r = jnp.where(lead, line_r[n : n + 1], p_r)
                        p_i = jnp.where(lead, line_i[n : n + 1], p_i)
                    prod[n, where, :L] = p_r.astype(BF)
                    prod[n, where, L:] = p_i.astype(BF)

    copies[tops].wait()
    copies[tops + 1].wait()
    products(0)
    copies[tops + 2].wait()
    copies[tops + 3].wait()
    for p in range(4):
        if p < 3:
            copies[tops + 4 + 2 * p].wait()
            copies[tops + 5 + 2 * p].wait()
            products(p + 1)
        middle = dot(prod[2 * p : 2 * p + 2].reshape(2 * H, 2 * L), cols[...]).astype(BF)
        kinds = []
        for c in range(2):
            both = []
            for k in range(2):
                part = middle[H * k + Q * c : H * k + Q * c + Q]
                both.append(jnp.concatenate([part[:, :L], part[:, L:]], 0))
            kinds.append(dot(rows[c], jnp.concatenate(both, 1)) * (1.0 / (L * L)))
        for at, corr in ((slice(0, H), kinds[0] + kinds[1]), (slice(H, L), kinds[0] - kinds[1])):
            one, two = corr[:, :L], corr[:, L:]
            largest = jnp.maximum(one, two)
            summed = one + two
            powers = one * one + two * two
            if p == 0:
                mip[at] = largest
                total[at] = summed
                square[at] = powers
            elif p < 3:
                mip[at] = jnp.maximum(mip[at], largest)
                total[at] += summed
                square[at] += powers
            else:
                largest = jnp.maximum(mip[at], largest)
                mean = (total[at] + summed) * 0.125
                var = (square[at] + powers) * 0.125 - mean * mean
                mip[at] = largest
                zmap[at] = (largest - mean) * lax.rsqrt(jnp.maximum(var, 0.25))


def search(spec, owns, others):
    held = pl.BlockSpec(memory_space=pltpu.HBM)
    return pl.pallas_call(
        search_kernel,
        out_shape=(jax.ShapeDtypeStruct((L, L), F32), jax.ShapeDtypeStruct((L, L), F32)),
        grid=(1,),
        in_specs=[held] + [pl.BlockSpec(memory_space=pl.ANY)] * 8 + [held] * 3,
        out_specs=[full_spec((L, L)), full_spec((L, L))],
        scratch_shapes=[
            pltpu.VMEM((2, H, L), BF),
            pltpu.VMEM((8, 2, Q, L), BF),
            pltpu.VMEM((8, 2, Q, L), BF),
            pltpu.VMEM((8, 2, 16, L), BF),
            pltpu.VMEM((8, 2, 16, L), BF),
            pltpu.VMEM((2 * L, 2 * L), BF),
            pltpu.VMEM((2, H, H), BF),
            pltpu.VMEM((L, L), BF),
            pltpu.VMEM((8, H, 2 * L), BF),
            pltpu.VMEM((L, L), F32),
            pltpu.VMEM((L, L), F32),
            pltpu.SemaphoreType.DMA((20,)),
        ],
        compiler_params=pltpu.CompilerParams(vmem_limit_bytes=56 * MB),
        cost_estimate=pl.CostEstimate(flops=4_000_000_000, bytes_accessed=6 * MB, transcendentals=0),
        name="search_templates",
    )(spec, *owns, *others, TAB["inverse_cols"], TAB["inverse_rows"], TAB["reverse"])


def ring(count, step):
    return [(i, (i + step) % count) for i in range(count)]


def z_ring(step):
    index = [(z % 2) * 2 + z // 2 for z in range(4)]
    return [(index[z], index[(z + step) % 4]) for z in range(4)]


def body(micrograph, templates, ref_bank, peak_offsets, peak_template, owners):
    def across(array):
        return lax.ppermute(array, "core", ring(2, 1))

    message, spec = prepare(
        peak_offsets.T, peak_template.reshape(1, 16), owners.reshape(1, 16), micrograph, ref_bank
    )
    arrived = lax.all_to_all(message, CHIPS, 0, 0, tiled=True)
    half = template_half(templates)
    along = [lax.ppermute(half, "y", ring(4, step)) for step in (1, 3, 2)]
    arrived, half, along = lax.optimization_barrier((arrived, half, along))
    lower, upper = jnp.stack([half, along[0]]), jnp.stack(along[1:])
    owns = [
        lower,
        upper,
        lax.ppermute(lower, ("zl", "zh"), z_ring(1)),
        lax.ppermute(upper, ("zl", "zh"), z_ring(3)),
    ]
    scores = refine(arrived, across(arrived))
    first = [across(one) for one in owns[:2]]
    after, last = lax.optimization_barrier((scores, owns[2:]))
    owns = owns[:2] + last
    returned = lax.all_to_all(scores.reshape(SLABS, 2, 128), CHIPS, 0, 0, tiled=True)
    mip, zmap = search(spec, owns, first + [across(one) for one in last])
    returned, mip, zmap, after = lax.optimization_barrier((returned, mip, zmap, after))
    refined = jnp.sum(returned, 0).reshape(16, 16)[:, :9]
    return (mip, zmap, refined)


def solution(mesh):
    inner = Mesh(mesh.devices.reshape(2, 4, 4, 2, 2), ("zl", "y", "x", "zh", "core"))
    every = ROWS_OF + COLS_OF
    placed = (
        P(ROWS_OF, COLS_OF),
        P(ROWS_OF, None, None),
        P(COLS_OF, None, None),
        P(every, None),
        P(every),
        P(every, None),
    )
    return jax.shard_map(
        body,
        mesh=inner,
        in_specs=placed,
        out_specs=(P(ROWS_OF, COLS_OF), P(ROWS_OF, COLS_OF), P(every, None)),
        check_vma=False,
    )
```

```python
import math

import jax
import jax.numpy as jnp
import numpy as np
from jax import lax
from jax.experimental import pallas as pl
from jax.experimental.pallas import tpu as pltpu
from jax.sharding import Mesh
from jax.sharding import PartitionSpec as P

L = 384
H = 192
Q = 96
SLABS = 64
ROWS = 40
WIDE = 1280
BF = jnp.bfloat16
F32 = jnp.float32
MB = 1024 * 1024
LIMIT = 62 * MB
ROWS_OF = ("zl", "y")
COLS_OF = ("x", "zh", "core")
CHIPS = ("zl", "y", "x", "zh")


def dot(a, b):
    return jnp.dot(a, b, preferred_element_type=F32)


def wave(a, b):
    angle = (np.multiply.outer(np.asarray(a), np.asarray(b)) % L) * (2.0 * math.pi / L)
    return np.cos(angle), np.sin(angle)


def bf(a):
    return np.asarray(a, np.float32).astype(jnp.bfloat16)


def make_tables():
    n = np.arange(L)
    cos, sin = wave(n, n)
    order = np.concatenate([np.arange(0, H, 2), np.arange(1, H, 2)])
    forward = np.concatenate([cos[order], cos[H : H + 1], sin[order[1:]]], 0)
    halves = np.stack(
        [np.concatenate([forward[c * Q : c * Q + Q], forward[H + c * Q : H + c * Q + Q]], 0) for c in range(2)]
    )
    pair = np.concatenate([cos, sin], 1)
    inverse_cols = np.concatenate([pair, np.concatenate([-sin, cos], 1)], 0)
    weight = np.full((H,), 2.0)
    weight[0] = 1.0
    back_cos, back_sin = cos[:H, order] * weight, -2.0 * sin[:H, order]
    back_sin[:, 0] = cos[:H, H]
    inverse_rows = np.stack(
        [np.concatenate([back_cos[:, Q * c : Q * c + Q], back_sin[:, Q * c : Q * c + Q]], 1) for c in range(2)]
    )
    reverse = np.zeros((L, L))
    reverse[(-n) % L, n] = 1.0
    pick = np.zeros((4, L, 128))
    for part in range(4):
        pick[part, n, 80 + 6 * part + n % 6] = 1.0
    lane = np.arange(128)
    field = np.zeros((128, 3, 128))
    for which, at in enumerate((0, 32, 64)):
        if which < 2:
            field[at : at + 16, which] = 128.0
            at += 16
        field[at : at + 16, which] = 1.0
    ac = lane % 16
    a, c = ac // 3 - 1, ac % 3 - 1
    comb = np.zeros((2, 3, L, 128))
    extra = np.zeros((SLABS, 2, 8, 128))
    for shift in (-1, 0, 1):
        kc, ks = wave(n, [shift])
        for part in range(4):
            at = 6 * part + 2 * (shift + 1)
            if part < 3:
                comb[0, part, :, at], comb[0, part, :, at + 1] = kc[:, 0], ks[:, 0]
                comb[1, part, :, at], comb[1, part, :, at + 1] = -ks[:, 0], kc[:, 0]
            else:
                kc, ks = kc[:, 0].reshape(SLABS, 6), ks[:, 0].reshape(SLABS, 6)
                extra[:, 0, :6, at], extra[:, 0, :6, at + 1] = kc, ks
                extra[:, 1, :6, at], extra[:, 1, :6, at + 1] = -ks, kc
    turn = np.zeros((SLABS, 16, L))
    widen = np.zeros((256, 16))
    last = np.zeros((SLABS, 2, 128, 128))
    for part in range(4):
        widen[6 * part : 6 * part + 6, part] = 1.0
        widen[128 + 6 * part : 128 + 6 * part + 6, 4 + part] = 1.0
    for s in range(SLABS):
        for part in range(4):
            k = order[s + 64 * part] if part < 3 else H
            kc, ks = wave([k], n)
            turn[s, part], turn[s, 4 + part] = kc[0], ks[0]
            ca, sa = wave([k], a)
            w = 1.0 if k in (0, H) else 2.0
            for shift in (-1, 0, 1):
                at = 6 * part + 2 * (shift + 1)
                on = w * ((ac < 9) & (c == shift))
                last[s, 0, at], last[s, 0, at + 1] = on * ca[0], -on * sa[0]
                last[s, 1, at], last[s, 1, at + 1] = -on * sa[0], -on * ca[0]
    tail = np.concatenate([reverse, inverse_rows.reshape(L, H), np.zeros((L, H))], 1)
    bundle = np.concatenate([inverse_cols, tail], 0)
    return dict(
        bundle=bf(bundle),
        forward=bf(forward),
        halves=bf(halves),
        pair=bf(pair),
        pick=bf(pick.reshape(4 * L, 128)),
        field=bf(field.reshape(128, 384)),
        comb=bf(comb.reshape(6 * L, 128)),
        extra=bf(extra.reshape(SLABS, 16, 128)),
        turn=bf(turn),
        widen=bf(widen),
        last=bf(last.reshape(SLABS, 256, 128)),
    )


TAB = make_tables()


def full_spec(shape):
    zeros = (0,) * len(shape)
    return pl.BlockSpec(shape, lambda i: zeros)


def place():
    blk = lax.axis_index("zl") * 4 + lax.axis_index("y")
    slab = blk * 8 + lax.axis_index("x") * 2 + lax.axis_index("zh")
    return blk, lax.axis_index("core"), slab


def iota(shape, dim):
    return lax.broadcasted_iota(jnp.int32, shape, dim)


def prepare_kernel(
    offsets,
    choice,
    owners,
    tile_hbm,
    bank_hbm,
    forward_hbm,
    pair_hbm,
    pick_hbm,
    msg,
    spec,
    flat,
    tile,
    ref,
    forward,
    pair,
    pick,
    sems,
):
    blk, core, _ = place()
    jobs = (
        (forward_hbm, forward),
        (tile_hbm, tile),
        (pair_hbm, pair),
        (bank_hbm.at[blk], ref),
        (pick_hbm, pick),
    )
    copies = [pltpu.make_async_copy(src, dst, sems.at[n]) for n, (src, dst) in enumerate(jobs)]
    for copy in copies:
        copy.start()

    r8 = iota((8, 16), 0)
    ox, oy = offsets[0:1], offsets[1:2]
    owner = owners[...]
    named = choice[...] * 8 + (owner >> 1) + 64 * ((owner & 1) ^ core)
    values = jnp.where(r8 == 4, named, 0)
    for n, value in enumerate((ox >> 7, ox & 127, oy >> 7, oy & 127)):
        values = jnp.where(r8 == n, value, values)
    wide = ((iota((16, 128), 1) & 15) == iota((16, 128), 0)).astype(BF)
    lined = dot(values.astype(F32).astype(BF), wide)
    lined = jnp.where((iota((8, 128), 1) >> 4) == iota((8, 128), 0), lined, 0.0)
    meta = jnp.sum(lined, axis=0, keepdims=True)

    rows64 = iota((SLABS, L), 0)
    owned = (iota((SLABS, L), 1) // 6) == rows64
    first_row = rows64 == 0
    for row in range(37, ROWS):
        flat[pl.ds(row, SLABS, stride=ROWS), :] = jnp.zeros((SLABS, 128), F32)
    copies[0].wait()
    lasts = []
    for which, image in enumerate((tile, ref)):
        copies[1 + 2 * which].wait()
        first = dot(forward[...], image[...]).astype(BF)
        if which == 0:
            copies[2].wait()
        second = dot(first, pair[...])
        real = second[:H, :L] - second[H:, L:]
        imag = -(second[:H, L:] + second[H:, :L])
        if which == 0:
            spec[0] = real.astype(BF)
            spec[1] = imag.astype(BF)
        for plane, (full, alone) in enumerate(((real, second[:64, :L]), (imag, -second[:64, L:]))):
            for part in range(3):
                block = full[64 * part : 64 * part + 64]
                if part == 0:
                    block = jnp.where(first_row, alone, block)
                for j in range(3):
                    row = 18 * which + 9 * plane + 3 * part + j
                    flat[pl.ds(row, SLABS, stride=ROWS), :] = block[:, 128 * j : 128 * j + 128]
        for last in (second[H : H + 1, :L], -second[H : H + 1, L:]):
            lasts.append(jnp.where(owned, jnp.broadcast_to(last, (SLABS, L)), 0.0).astype(BF))
    copies[4].wait()
    line = dot(jnp.concatenate(lasts, 1), pick[...])
    flat[pl.ds(36, SLABS, stride=ROWS), :] = line + meta
    msg[...] = flat[...].reshape(SLABS, ROWS, 128).astype(BF)


def prepare(offsets, choice, owners, tile, bank):
    held = pl.BlockSpec(memory_space=pltpu.HBM)
    return pl.pallas_call(
        prepare_kernel,
        out_shape=(
            jax.ShapeDtypeStruct((SLABS, ROWS, 128), BF),
            jax.ShapeDtypeStruct((2, H, L), BF),
        ),
        grid=(1,),
        in_specs=[full_spec((2, 16)), full_spec((1, 16)), full_spec((1, 16))] + [held] * 5,
        out_specs=[full_spec((SLABS, ROWS, 128)), full_spec((2, H, L))],
        scratch_shapes=[
            pltpu.VMEM((SLABS * ROWS, 128), F32),
            pltpu.VMEM((L, L), BF),
            pltpu.VMEM((L, L), BF),
            pltpu.VMEM((L, L), BF),
            pltpu.VMEM((L, 2 * L), BF),
            pltpu.VMEM((4 * L, 128), BF),
            pltpu.SemaphoreType.DMA((5,)),
        ],
        compiler_params=pltpu.CompilerParams(vmem_limit_bytes=62 * MB),
        cost_estimate=pl.CostEstimate(flops=1_000_000_000, bytes_accessed=4 * MB, transcendentals=0),
        name="prepare_spectra",
    )(offsets, choice, owners, tile, bank, TAB["forward"], TAB["pair"], TAB["pick"])


def template_kernel(template_hbm, halves_hbm, pair_hbm, half, template, rows_half, pair, sems):
    core = lax.axis_index("core")
    jobs = ((template_hbm.at[0], template), (halves_hbm.at[core], rows_half), (pair_hbm, pair))
    copies = [pltpu.make_async_copy(src, dst, sems.at[n]) for n, (src, dst) in enumerate(jobs)]
    for copy in copies:
        copy.start()
    copies[0].wait()
    values = template[...].astype(F32)
    count = 1.0 / (L * L)
    spread = values - jnp.sum(values) * count
    power = jnp.sum(spread * spread) * count
    scale = 1.0 / (L * jnp.sqrt(jnp.full((1, 1), power + 1e-06, F32)))
    normalized = (spread * scale).astype(BF)
    copies[1].wait()
    first = dot(rows_half[...], normalized).astype(BF)
    copies[2].wait()
    second = dot(first, pair[...])
    half[0] = (second[:Q, :L] - second[Q:, L:]).astype(BF)
    half[1] = (-(second[:Q, L:] + second[Q:, :L])).astype(BF)


def template_half(templates):
    held = pl.BlockSpec(memory_space=pltpu.HBM)
    return pl.pallas_call(
        template_kernel,
        out_shape=jax.ShapeDtypeStruct((2, Q, L), BF),
        grid=(1,),
        in_specs=[held] * 3,
        out_specs=full_spec((2, Q, L)),
        scratch_shapes=[
            pltpu.VMEM((L, L), BF),
            pltpu.VMEM((H, L), BF),
            pltpu.VMEM((L, 2 * L), BF),
            pltpu.SemaphoreType.DMA((3,)),
        ],
        compiler_params=pltpu.CompilerParams(vmem_limit_bytes=36 * MB),
        cost_estimate=pl.CostEstimate(flops=400_000_000, bytes_accessed=4 * MB, transcendentals=0),
        name="template_spectrum",
    )(templates, TAB["halves"], TAB["pair"])


MAIN = 6 * L
N_CAND = 1024


def refine_kernel(
    own_hbm, other_hbm, pair_hbm, field_hbm, comb_hbm, widen_hbm, turn_hbm, extra_hbm, last_hbm, out,
    own, other, pair, field, comb, widen, turn, extra, last,
    flat, tiles, refs, waves, ref_of, wave_of, both, turned, sems,
):
    slab = place()[2]
    jobs = (
        (pair_hbm, pair),
        (widen_hbm, widen),
        (turn_hbm.at[pl.ds(slab, 1)], turn),
        (extra_hbm.at[pl.ds(slab, 1)], extra),
        (other_hbm, other),
        (own_hbm, own),
        (field_hbm, field),
        (comb_hbm, comb),
        (last_hbm.at[pl.ds(slab, 1)], last),
    )
    copies = [pltpu.make_async_copy(src, dst, sems.at[n]) for n, (src, dst) in enumerate(jobs)]
    for copy in copies:
        copy.start()
    lane64 = iota((SLABS, 128), 1)

    def spread(base, target, rows):
        for col in range(18):
            target[rows, 128 * col : 128 * col + 128] = flat[pl.ds(base + col, SLABS, stride=ROWS), :].astype(
                target.dtype
            )
        line = flat[pl.ds(36, SLABS, stride=ROWS), :]
        for plane in range(2):
            at = 80 + (12 if base else 0) + 6 * plane
            moved = jnp.where(lane64 < 6, pltpu.roll(line, 128 - at, axis=1), 0.0)
            target[rows, MAIN + 128 * plane : MAIN + 128 * plane + 128] = moved.astype(target.dtype)
        return line

    copies[0].wait()
    waves[:, : 2 * L] = pair[...]
    wanted = (iota((L, 128), 0) == iota((L, 128), 1) + 6 * slab).astype(BF)
    waves[:, 768:896] = dot(pair[:, :L], wanted).astype(BF)
    waves[:, 896:1024] = dot(pair[:, L:], wanted).astype(BF)
    copies[1].wait()
    copies[2].wait()
    copies[3].wait()
    turns = dot(widen[...], turn[0]).astype(BF)
    pad = jnp.zeros((112, 128), BF)
    ends = jnp.concatenate(
        [
            jnp.concatenate([extra[0, :8].astype(F32), jnp.zeros((8, 128), F32)], 0).astype(BF),
            pad,
            jnp.concatenate([extra[0, 8:].astype(F32), jnp.zeros((8, 128), F32)], 0).astype(BF),
            pad,
        ],
        0,
    )

    copies[4].wait()
    flat[...] = other[...].astype(F32).reshape(SLABS * ROWS, 128)
    spread(18, refs, slice(64, 128))
    copies[5].wait()
    flat[...] = own[...].astype(F32).reshape(SLABS * ROWS, 128)
    spread(18, refs, slice(0, 64))
    meta = spread(0, tiles, slice(0, 64)).astype(BF)

    block = 256
    rowb = iota((block, 128), 0)
    laneb = iota((block, 128), 1)
    mine = (laneb & 15) == (rowb & 15)
    lanef = laneb.astype(F32)

    def gather(q):
        rows = pl.ds(block * q, block)
        repeat = iota((block, SLABS), 1) == 16 * q + (iota((block, SLABS), 0) >> 4)
        fields = dot(repeat.astype(BF), meta)
        spots = dot(jnp.where(mine, fields, 0.0).astype(BF), field[...])
        hot_x = jnp.concatenate([(lanef + 128.0 * j == spots[:, :128]).astype(BF) for j in range(3)], 1)
        hot_y = jnp.concatenate([(lanef + 128.0 * j == spots[:, 128:256]).astype(BF) for j in range(3)], 1)
        hot_t = (lanef == spots[:, 256:]).astype(BF)
        ref_of[rows, :] = dot(hot_t, refs[...])
        wave_of[rows, :] = dot(hot_y, waves[...])
        turned[rows, :] = lax.dot_general(
            hot_x, turns, (((1,), (1,)), ((), ())), preferred_element_type=F32
        ).astype(BF)

    def multiply(q):
        for size, wave_at, places in (
            (L, 0, tuple((L * part, 3 * L + L * part) for part in range(3))),
            (128, 2 * L, ((MAIN, MAIN + 128),)),
        ):
            for j in range(8):
                rows = pl.ds(128 * q + 16 * j, 16)
                for m in range(0, size, 128):
                    cos_y = wave_of[rows, wave_at + m : wave_at + m + 128].astype(F32)
                    sin_y = wave_of[rows, wave_at + size + m : wave_at + size + m + 128].astype(F32)
                    for at_r, at_i in places:
                        lanes_r, lanes_i = slice(at_r + m, at_r + m + 128), slice(at_i + m, at_i + m + 128)
                        tile_r = tiles[8 * q + j : 8 * q + j + 1, lanes_r]
                        tile_i = tiles[8 * q + j : 8 * q + j + 1, lanes_i]
                        ref_r = ref_of[rows, lanes_r].astype(F32)
                        ref_i = ref_of[rows, lanes_i].astype(F32)
                        prod_r = tile_r * ref_r + tile_i * ref_i
                        prod_i = tile_i * ref_r - tile_r * ref_i
                        both[rows, lanes_r] = (prod_r * cos_y - prod_i * sin_y).astype(BF)
                        both[rows, lanes_i] = (prod_r * sin_y + prod_i * cos_y).astype(BF)

    kept = (laneb >> 4) == (rowb & 7)

    def finish(q):
        rows = pl.ds(block * q, block)
        sums = dot(both[rows, :MAIN], comb[...]) + dot(both[rows, MAIN:], ends)
        kappa = turned[rows, :].astype(F32)
        mixed = jnp.concatenate([(sums * kappa[:, :128]).astype(BF), (sums * kappa[:, 128:]).astype(BF)], 1)
        total = jnp.where(kept, dot(mixed, last[0]) * (1.0 / (L * L)), 0.0)
        to = pl.ds(block // 8 * q, block // 8)
        out[to, :] = jnp.sum(total.reshape(block // 8, 8, 128), axis=1)

    count = N_CAND // block
    for n in (6, 7, 8):
        copies[n].wait()
    gather(0)
    for q in range(count):
        if q + 1 < count:
            gather(q + 1)
        for p in range(block // 128):
            multiply(block // 128 * q + p)
        finish(q)


def refine(own, other):
    held = pl.BlockSpec(memory_space=pltpu.HBM)
    return pl.pallas_call(
        refine_kernel,
        out_shape=jax.ShapeDtypeStruct((128, 128), F32),
        grid=(1,),
        in_specs=[pl.BlockSpec(memory_space=pl.ANY)] * 2 + [held] * 7,
        out_specs=full_spec((128, 128)),
        scratch_shapes=[
            pltpu.VMEM((SLABS, ROWS, 128), BF),
            pltpu.VMEM((SLABS, ROWS, 128), BF),
            pltpu.VMEM((L, 2 * L), BF),
            pltpu.VMEM((128, 384), BF),
            pltpu.VMEM((MAIN, 128), BF),
            pltpu.VMEM((256, 16), BF),
            pltpu.VMEM((1, 16, L), BF),
            pltpu.VMEM((1, 16, 128), BF),
            pltpu.VMEM((1, 256, 128), BF),
            pltpu.VMEM((SLABS * ROWS, 128), F32),
            pltpu.VMEM((SLABS, MAIN + 256), F32),
            pltpu.VMEM((128, MAIN + 256), BF),
            pltpu.VMEM((L, 1024), BF),
            pltpu.VMEM((N_CAND, MAIN + 256), F32),
            pltpu.VMEM((N_CAND, 1024), F32),
            pltpu.VMEM((N_CAND, MAIN + 256), BF),
            pltpu.VMEM((N_CAND, 256), BF),
            pltpu.SemaphoreType.DMA((9,)),
        ],
        compiler_params=pltpu.CompilerParams(vmem_limit_bytes=62 * MB),
        cost_estimate=pl.CostEstimate(flops=9_000_000_000, bytes_accessed=4 * MB, transcendentals=0),
        name="refine_slab",
    )(own, other, TAB["pair"], TAB["field"], TAB["comb"], TAB["widen"], TAB["turn"], TAB["extra"], TAB["last"])


def search_kernel(
    spec_hbm, o0, o1, o2, o3, p0, p1, p2, p3, bundle_hbm, mip, zmap,
    spec, own, oth, own_top, oth_top, cols, rows, reverse, prod, total, square, sems,
):
    core = lax.axis_index("core")
    owns, others = (o0, o1, o2, o3), (p0, p1, p2, p3)
    lower = pl.ds(2 * L, L)
    jobs = [(spec_hbm, spec), (bundle_hbm.at[lower, pl.ds(0, L)], reverse)]
    for p in range(4):
        jobs.append((owns[p].at[:, :, pl.ds(0, 16), :], own_top.at[pl.ds(2 * p, 2)]))
        jobs.append((others[p].at[:, :, pl.ds(0, 16), :], oth_top.at[pl.ds(2 * p, 2)]))
    tops = len(jobs)
    for p in range(4):
        jobs.append((owns[p], own.at[pl.ds(2 * p, 2)]))
        jobs.append((others[p], oth.at[pl.ds(2 * p, 2)]))
        if p == 0:
            jobs += [(bundle_hbm.at[pl.ds(0, 2 * L)], cols), (bundle_hbm.at[lower, pl.ds(L, 256)], rows)]
    copies = [pltpu.make_async_copy(src, dst, sems.at[n]) for n, (src, dst) in enumerate(jobs)]
    for copy in copies:
        copy.start()

    row16 = iota((16, L), 0)
    zero = jnp.zeros((16, L), F32)
    ends_r, ends_i = zero, zero
    for n in range(tops):
        copies[n].wait()
    for n in range(8):
        top_r = jnp.where(core == 0, own_top[n, 0].astype(F32), oth_top[n, 0].astype(F32))
        top_i = jnp.where(core == 0, own_top[n, 1].astype(F32), oth_top[n, 1].astype(F32))
        ends_r = jnp.where(row16 == n, top_r[0:1], ends_r)
        ends_i = jnp.where(row16 == n, top_i[0:1], ends_i)
    ends_r = jnp.where(row16 == 8, spec[0, :16].astype(F32)[0:1], ends_r)
    ends_i = jnp.where(row16 == 8, spec[1, :16].astype(F32)[0:1], ends_i)
    back = dot(jnp.concatenate([ends_r, ends_i], 0).astype(BF), reverse[...])
    back_r, back_i = back[:16], back[16:]
    low_r, low_i = 0.5 * (ends_r + back_r), 0.5 * (ends_i - back_i)
    top_r, top_i = -0.5 * (ends_i + back_i), 0.5 * (ends_r - back_r)

    def cross(a_r, a_i):
        s_r, s_i = a_r[8:9], a_i[8:9]
        return s_r * a_r + s_i * a_i, s_i * a_r - s_r * a_i

    low = cross(low_r, low_i)
    top = cross(top_r, top_i)
    line_r = low[0] - top[1]
    line_i = low[1] + top[0]

    def products(p):
        for n in (2 * p, 2 * p + 1):
            for ref, half in ((own, core), (oth, 1 - core)):
                for r in range(0, Q, 16):
                    where = pl.ds(pl.multiple_of(half * Q + r, 16), 16)
                    tile_r, tile_i = spec[0, where, :].astype(F32), spec[1, where, :].astype(F32)
                    t_r, t_i = ref[n, 0, r : r + 16].astype(F32), ref[n, 1, r : r + 16].astype(F32)
                    p_r = tile_r * t_r + tile_i * t_i
                    p_i = tile_i * t_r - tile_r * t_i
                    if r == 0:
                        lead = (row16 + half) == 0
                        p_r = jnp.where(lead, line_r[n : n + 1], p_r)
                        p_i = jnp.where(lead, line_i[n : n + 1], p_i)
                    prod[n, where, :L] = p_r.astype(BF)
                    prod[n, where, L:] = p_i.astype(BF)

    copies[tops].wait()
    copies[tops + 1].wait()
    products(0)
    copies[tops + 2].wait()
    copies[tops + 3].wait()
    for p in range(4):
        if p < 3:
            copies[tops + 4 + 2 * p].wait()
            copies[tops + 5 + 2 * p].wait()
            products(p + 1)
        middle = dot(prod[2 * p : 2 * p + 2].reshape(2 * H, 2 * L), cols[...]).astype(BF)
        kinds = []
        for c in range(2):
            both = []
            for k in range(2):
                part = middle[H * k + Q * c : H * k + Q * c + Q]
                both.append(jnp.concatenate([part[:, :L], part[:, L:]], 0))
            kinds.append(dot(rows[H * c : H * c + H, :H], jnp.concatenate(both, 1)) * (1.0 / (L * L)))
        for at, corr in ((slice(0, H), kinds[0] + kinds[1]), (slice(H, L), kinds[0] - kinds[1])):
            one, two = corr[:, :L], corr[:, L:]
            largest = jnp.maximum(one, two)
            summed = one + two
            powers = one * one + two * two
            if p == 0:
                mip[at] = largest
                total[at] = summed
                square[at] = powers
            elif p < 3:
                mip[at] = jnp.maximum(mip[at], largest)
                total[at] += summed
                square[at] += powers
            else:
                largest = jnp.maximum(mip[at], largest)
                mean = (total[at] + summed) * 0.125
                var = (square[at] + powers) * 0.125 - mean * mean
                mip[at] = largest
                zmap[at] = (largest - mean) * lax.rsqrt(jnp.maximum(var, 0.25))


def search(spec, owns, others):
    held = pl.BlockSpec(memory_space=pltpu.HBM)
    return pl.pallas_call(
        search_kernel,
        out_shape=(jax.ShapeDtypeStruct((L, L), F32), jax.ShapeDtypeStruct((L, L), F32)),
        grid=(1,),
        in_specs=[held] + [pl.BlockSpec(memory_space=pl.ANY)] * 8 + [held],
        out_specs=[full_spec((L, L)), full_spec((L, L))],
        scratch_shapes=[
            pltpu.VMEM((2, H, L), BF),
            pltpu.VMEM((8, 2, Q, L), BF),
            pltpu.VMEM((8, 2, Q, L), BF),
            pltpu.VMEM((8, 2, 16, L), BF),
            pltpu.VMEM((8, 2, 16, L), BF),
            pltpu.VMEM((2 * L, 2 * L), BF),
            pltpu.VMEM((L, 256), BF),
            pltpu.VMEM((L, L), BF),
            pltpu.VMEM((8, H, 2 * L), BF),
            pltpu.VMEM((L, L), F32),
            pltpu.VMEM((L, L), F32),
            pltpu.SemaphoreType.DMA((20,)),
        ],
        compiler_params=pltpu.CompilerParams(vmem_limit_bytes=46 * MB),
        cost_estimate=pl.CostEstimate(flops=4_000_000_000, bytes_accessed=6 * MB, transcendentals=0),
        name="search_templates",
    )(spec, *owns, *others, TAB["bundle"])


def ring(count, step):
    return [(i, (i + step) % count) for i in range(count)]


def z_ring(step):
    index = [(z % 2) * 2 + z // 2 for z in range(4)]
    return [(index[z], index[(z + step) % 4]) for z in range(4)]


def body(micrograph, templates, ref_bank, peak_offsets, peak_template, owners):
    def across(array):
        return lax.ppermute(array, "core", ring(2, 1))

    message, spec = prepare(
        peak_offsets.T, peak_template.reshape(1, 16), owners.reshape(1, 16), micrograph, ref_bank
    )
    arrived = lax.all_to_all(message, CHIPS, 0, 0, tiled=True)
    half = template_half(templates)
    along = [lax.ppermute(half, "y", ring(4, step)) for step in (1, 3, 2)]
    arrived, half, along = lax.optimization_barrier((arrived, half, along))
    lower, upper = jnp.stack([half, along[0]]), jnp.stack(along[1:])
    owns = [
        lower,
        upper,
        lax.ppermute(lower, ("zl", "zh"), z_ring(1)),
        lax.ppermute(upper, ("zl", "zh"), z_ring(3)),
    ]
    scores = refine(arrived, across(arrived))
    first = [across(one) for one in owns[:2]]
    after, last = lax.optimization_barrier((scores, owns[2:]))
    owns = owns[:2] + last
    returned = lax.all_to_all(scores.reshape(SLABS, 2, 128), CHIPS, 0, 0, tiled=True)
    mip, zmap = search(spec, owns, first + [across(one) for one in last])
    returned, mip, zmap, after = lax.optimization_barrier((returned, mip, zmap, after))
    refined = jnp.sum(returned, 0).reshape(16, 16)[:, :9]
    return (mip, zmap, refined)


def solution(mesh):
    inner = Mesh(mesh.devices.reshape(2, 4, 4, 2, 2), ("zl", "y", "x", "zh", "core"))
    every = ROWS_OF + COLS_OF
    placed = (
        P(ROWS_OF, COLS_OF),
        P(ROWS_OF, None, None),
        P(COLS_OF, None, None),
        P(every, None),
        P(every),
        P(every, None),
    )
    return jax.shard_map(
        body,
        mesh=inner,
        in_specs=placed,
        out_specs=(P(ROWS_OF, COLS_OF), P(ROWS_OF, COLS_OF), P(every, None)),
        check_vma=False,
    )
```
